256 devices in a mesh: grp: 16 (over z, core), dev: 16 (over y, x).
Axes of the slice: x: 4, y: 4, z: 8, core: 2. Of those that a mesh axis runs over, the one named last changes fastest.
Arguments:
- voxel_features: float32 [1024, 64, 512], P(('grp', 'dev')), may hold values from -6 to 6
- fine_links: int32 [1024, 26], P(('grp', 'dev')), may hold values from -1 to 1023, as said below
- parent_codes: int32 [1024], P(('grp', 'dev')), may hold values from 0 to 255, as said below
- coarse_links: int32 [512, 26], P(('grp', 'dev')), may hold values from -1 to 511, as said below
- fine_in_weight: float32 [64, 1728], replicated, may hold values from -0.15625 to 0.15625
- fine_in_bias: float32 [64], replicated, may hold values from -3 to 3
- down_weight: float32 [128, 64], replicated, may hold values from -0.75 to 0.75
- coarse_first_weight: float32 [128, 3456], replicated, may hold values from -0.109375 to 0.109375
- coarse_first_bias: float32 [128], replicated, may hold values from -3 to 3
- coarse_second_weight: float32 [128, 3456], replicated, may hold values from -0.109375 to 0.109375
- coarse_second_bias: float32 [128], replicated, may hold values from -3 to 3
- up_weight: float32 [64, 128], replicated, may hold values from -0.5 to 0.5
- fine_out_weight: float32 [64, 1728], replicated, may hold values from -0.15625 to 0.15625
- fine_out_bias: float32 [64], replicated, may hold values from -3 to 3
Outputs:
- refined: float32 [1024, 64, 512], P(('grp', 'dev'))
The draws below stay inside these ranges and needn't reach their ends.
Inputs may be any that keep to these rules, and one draw needn't show every extreme that they name: `fine_links`: devices are numbered along grp then dev, device d holding bricks d * 4 to (d + 1) * 4 - 1. An entry is -1 or a brick from d * 4 - 2 to (d + 1) * 4 + 1 for a brick of device d, with 2 = 2. parent_codes[i] = 8 * 2 * owner + 8 * slot + octant: owner is the dev index, within the brick's group of 16 devices, of the device that holds the parent, slot the parent's slot there (0 to 1), and octant = 4 * a + 2 * b + c the child's octant. Within a group all codes differ; the number of slots in use differs from device to device, and some device of every group uses all 2. `coarse_links`: device d holds slots d * 2 to (d + 1) * 2 - 1. An entry is -1 or a slot from (d - 1) * 2 to (d + 2) * 2 - 1 for a slot of device d.
All inputs are finite; a program needn't handle non-finite values.
Results may differ from the reference program's by a relative error of at most 0.0001.
Values sent between devices are 32-bit elements; how exact they have to be, the bound alone decides.
No kernel may reach another device: no remote copies, remote signals or barrier semaphores. Data moves between devices by JAX's collectives and lax.ppermute only.
A program may use at most 128 MiB of HBM per device.

```python
import jax
import jax.numpy as jnp
from jax import lax

CF = 64
CC = 128
BR = 4
CMAX = 2
HALO = 2
NB = 1024
NCS = 512
N_GRP = 16
N_DEV = 16


def nearby_links(key, row_total, run_length, reach_low, reach_high):
    positions = jnp.arange(row_total, dtype=jnp.int32)
    first_slot = positions // run_length * run_length
    key_offset, key_keep = jax.random.split(key)
    offsets = jax.random.randint(key_offset, (row_total, 26), -reach_low, run_length + reach_high, dtype=jnp.int32)
    targets = jnp.clip(first_slot[:, None] + offsets, 0, row_total - 1)
    kept_mask = jax.random.randint(key_keep, (row_total, 26), 0, 10, dtype=jnp.int32) < 7
    return jnp.where(kept_mask, targets, -1).astype(jnp.int32)


def draw_fine_links(key, part):
    return nearby_links(jax.random.fold_in(key, 11), NB, BR, HALO, HALO)


def draw_coarse_links(key, part):
    return nearby_links(jax.random.fold_in(key, 12), NCS, CMAX, CMAX, CMAX)


def draw_parent_codes(key, part):
    key_live, key_pick, key_score = jax.random.split(jax.random.fold_in(key, 13), 3)
    fewest = (BR + 7) // 8
    live_slots = jax.random.randint(key_live, (N_GRP, N_DEV), fewest, CMAX + 1, dtype=jnp.int32)
    chosen = jax.random.randint(key_pick, (N_GRP, 1), 0, N_DEV, dtype=jnp.int32)
    live_slots = jnp.where(jnp.arange(N_DEV, dtype=jnp.int32)[None, :] == chosen, CMAX, live_slots)
    code_total = N_DEV * CMAX * 8
    code_ids = jnp.arange(code_total, dtype=jnp.int32)
    owners = code_ids // (CMAX * 8)
    slot_ids = code_ids // 8 % CMAX
    alive_codes = slot_ids[None, :] < live_slots[:, owners]
    scores = jax.random.randint(key_score, (N_GRP, code_total), 0, 2 ** 20, dtype=jnp.int32)
    scores = scores + jnp.where(alive_codes, 0, 2 ** 21)
    ranked = jnp.argsort(scores * code_total + code_ids[None, :], axis=1)
    return ranked[:, :N_DEV * BR].reshape(-1).astype(jnp.int32)


def levels(stream_key, dims, cuts, low, largest):
    loudness = 1.0
    for axis_at, blocks in cuts:
        steps = jax.random.uniform(jax.random.fold_in(jax.random.fold_in(stream_key, 6), axis_at), (blocks,), jnp.float32, low / len(cuts), largest / len(cuts))
        loudness = loudness * jnp.repeat(jnp.exp(steps), dims[axis_at] // blocks).reshape((-1,) + (1,) * (len(dims) - 1 - axis_at))
    return loudness


def scatter_about(rng, shape, spread, reach, cuts=(), kind=jnp.bfloat16):
    array = jax.random.normal(rng, shape, jnp.float32) * spread
    if len(cuts) > 0:
        array = levels(rng, shape, cuts, -0.22, 0.18) * array
    return jnp.clip(array, min=-reach, max=reach).astype(kind)


def setup_inputs(seed: int = 0) -> dict:
    key_list = jax.random.split(jax.random.key(seed), 15)
    voxel_features = scatter_about(key_list[0], (NB, CF, 512), 1.0, 6.0, ((0, 256),), jnp.float32)
    fine_links = draw_fine_links(jax.random.fold_in(key_list[14], 71), 0)
    parent_codes = draw_parent_codes(jax.random.fold_in(key_list[14], 71), 0)
    coarse_links = draw_coarse_links(jax.random.fold_in(key_list[14], 71), 0)
    fine_in_weight = scatter_about(key_list[4], (CF, 27 * CF), (27 * CF) ** -0.5, 0.15625, (), jnp.float32)
    fine_in_bias = scatter_about(key_list[5], (CF,), 0.5, 3.0, (), jnp.float32)
    down_weight = scatter_about(key_list[6], (CC, CF), CF ** -0.5, 0.75, (), jnp.float32)
    coarse_first_weight = scatter_about(key_list[7], (CC, 27 * CC), (27 * CC) ** -0.5, 0.109375, (), jnp.float32)
    coarse_first_bias = scatter_about(key_list[8], (CC,), 0.5, 3.0, (), jnp.float32)
    coarse_second_weight = scatter_about(key_list[9], (CC, 27 * CC), (27 * CC) ** -0.5, 0.109375, (), jnp.float32)
    coarse_second_bias = scatter_about(key_list[10], (CC,), 0.5, 3.0, (), jnp.float32)
    up_weight = scatter_about(key_list[11], (CF, CC), CC ** -0.5, 0.5, (), jnp.float32)
    fine_out_weight = scatter_about(key_list[12], (CF, 27 * CF), (27 * CF) ** -0.5, 0.15625, (), jnp.float32)
    fine_out_bias = scatter_about(key_list[13], (CF,), 0.5, 3.0, (), jnp.float32)
    return {"voxel_features": voxel_features, "fine_links": fine_links, "parent_codes": parent_codes, "coarse_links": coarse_links, "fine_in_weight": fine_in_weight, "fine_in_bias": fine_in_bias, "down_weight": down_weight, "coarse_first_weight": coarse_first_weight, "coarse_first_bias": coarse_first_bias, "coarse_second_weight": coarse_second_weight, "coarse_second_bias": coarse_second_bias, "up_weight": up_weight, "fine_out_weight": fine_out_weight, "fine_out_bias": fine_out_bias}


neighbour_offsets = [(step_x, step_y, step_z) for step_x in (-1, 0, 1) for step_y in (-1, 0, 1) for step_z in (-1, 0, 1) if (step_x, step_y, step_z) != (0, 0, 0)]
source_planes = {-1: slice(7, 8), 0: slice(0, 8), 1: slice(0, 1)}


def assemble(source, center, links):
    extent = source.shape[0]
    bricks = center.shape[0]
    channels = center.shape[1]
    bricks_ext = jnp.concatenate([source, jnp.zeros((1,) + source.shape[1:], source.dtype)], 0)
    bricks_ext = bricks_ext.reshape(extent + 1, channels, 8, 8, 8)
    picked = jnp.where(links < 0, extent, links).astype(jnp.int32)
    middle = center.reshape(bricks, channels, 8, 8, 8)
    slabs = []
    for step_x in (-1, 0, 1):
        rows = []
        for step_y in (-1, 0, 1):
            cells = []
            for step_z in (-1, 0, 1):
                if (step_x, step_y, step_z) == (0, 0, 0):
                    cells.append(middle)
                else:
                    column = neighbour_offsets.index((step_x, step_y, step_z))
                    planes = bricks_ext[:, :, source_planes[step_x], source_planes[step_y], source_planes[step_z]]
                    cells.append(planes[picked[:, column]])
            rows.append(jnp.concatenate(cells, axis=4))
        slabs.append(jnp.concatenate(rows, axis=3))
    return jnp.concatenate(slabs, axis=2)


def convolve(source, center, links, weight, biases):
    padded = assemble(source, center, links)
    bricks = center.shape[0]
    channels = center.shape[1]
    summed = jnp.zeros((bricks, weight.shape[0], 512), jnp.float32)
    for offset_x in range(3):
        windows = []
        for offset_y in range(3):
            for offset_z in range(3):
                windows.append(padded[:, :, offset_x:offset_x + 8, offset_y:offset_y + 8, offset_z:offset_z + 8].reshape(bricks, channels, 512))
        stacked = jnp.concatenate(windows, axis=1)
        kernel = weight[:, 9 * offset_x * channels:(9 * offset_x + 9) * channels]
        summed = summed + jnp.einsum("oc,bcv->bov", kernel, stacked, precision=lax.Precision.HIGHEST)
    return summed + biases[None, :, None]


def pooling(hidden):
    bricks = hidden.shape[0]
    channels = hidden.shape[1]
    return hidden.reshape(bricks, channels, 4, 2, 4, 2, 4, 2).sum(axis=(3, 5, 7)).reshape(bricks, channels * 64) * 0.125


def octants_to_bricks(pieces, channels):
    slots = pieces.shape[0] // 8
    return pieces.reshape(slots, 2, 2, 2, channels, 4, 4, 4).transpose(0, 4, 1, 5, 2, 6, 3, 7).reshape(slots, channels, 512)


def bricks_to_octants(cubes, channels):
    slots = cubes.shape[0]
    return cubes.reshape(slots, channels, 2, 4, 2, 4, 2, 4).transpose(0, 2, 4, 6, 1, 3, 5, 7).reshape(slots * 8, channels * 64)


def upsample(octants, channels):
    bricks = octants.shape[0]
    grown = jnp.broadcast_to(octants.reshape(bricks, channels, 4, 1, 4, 1, 4, 1), (bricks, channels, 4, 2, 4, 2, 4, 2))
    return grown.reshape(bricks, channels, 512)


def reference(voxel_features, fine_links, parent_codes, coarse_links, fine_in_weight, fine_in_bias, down_weight, coarse_first_weight, coarse_first_bias, coarse_second_weight, coarse_second_bias, up_weight, fine_out_weight, fine_out_bias):
    bricks = voxel_features.shape[0]
    channels = voxel_features.shape[1]
    hidden = jax.nn.silu(convolve(voxel_features, voxel_features, fine_links, fine_in_weight, fine_in_bias))
    pooled = pooling(hidden)
    groups = jnp.arange(bricks, dtype=jnp.int32) // (N_DEV * BR)
    parent_rows = (groups * (N_DEV * CMAX * 8) + parent_codes.astype(jnp.int32)).astype(jnp.int32)
    slot_total = coarse_links.shape[0]
    pieces = jnp.zeros((slot_total * 8, channels * 64), jnp.float32).at[parent_rows].set(pooled)
    coarse_in = octants_to_bricks(pieces, channels)
    coarse_base = jnp.einsum("oc,bcv->bov", down_weight, coarse_in, precision=lax.Precision.HIGHEST)
    coarse_first = jax.nn.silu(convolve(coarse_base, coarse_base, coarse_links, coarse_first_weight, coarse_first_bias))
    coarse_second = jax.nn.silu(convolve(coarse_first, coarse_first, coarse_links, coarse_second_weight, coarse_second_bias))
    lifted = jnp.einsum("oc,bcv->bov", up_weight, coarse_second, precision=lax.Precision.HIGHEST)
    upward = bricks_to_octants(lifted, channels)
    rising = upsample(upward[parent_rows], channels)
    blended = jax.nn.silu(hidden + rising)
    return voxel_features + convolve(blended, blended, fine_links, fine_out_weight, fine_out_bias)
```

```python
import jax
import jax.numpy as jnp
from jax import lax
from jax.experimental import pallas as pl
from jax.experimental.pallas import tpu as pltpu
from jax.sharding import PartitionSpec as P

F32, BF16 = jnp.float32, jnp.bfloat16
BOTH = ("grp", "dev")
STEPS = (-1, 0, 1)
COLUMN = {
    offset: k
    for k, offset in enumerate(
        (x, y, z) for x in STEPS for y in STEPS for z in STEPS if (x, y, z) != (0, 0, 0)
    )
}
PLANE = {-1: slice(7, 8), 0: slice(0, 8), 1: slice(0, 1)}
ROOM = {-1: slice(0, 1), 0: slice(1, 9), 1: slice(9, 10)}
VMEM = pl.BlockSpec(memory_space=pltpu.VMEM)
SMEM = pl.BlockSpec(memory_space=pltpu.SMEM)


def silu(v):
    return v / (1.0 + jnp.exp(-v))


def split(v):
    high = v.astype(BF16)
    return high, (v - high.astype(F32)).astype(BF16)


def low_lanes(shape):
    return lax.broadcasted_iota(jnp.int32, shape, len(shape) - 1) < 64


def swap(v):
    return pltpu.roll(v, 64, v.ndim - 1)


def device_number():
    return lax.axis_index("grp") * lax.axis_size("dev") + lax.axis_index("dev")


def neighbours(links_ref, row, start, none):
    found = {}
    for offset, k in COLUMN.items():
        link = links_ref[row, k]
        found[offset] = jnp.where(link < 0, none, link - start)
    return found


def shifted_rows(tile):
    below, here, above = tile(-1), tile(0), tile(1)
    axis = here.ndim - 2
    row = lax.broadcasted_iota(jnp.int32, here.shape, axis)
    return (
        pltpu.roll(jnp.where(row == 7, below, here), 1, axis),
        here,
        pltpu.roll(jnp.where(row == 0, above, here), 7, axis),
    )


def product(high, low, weight_ref):
    both = jnp.dot(high, weight_ref[...], preferred_element_type=F32)
    half = both.shape[1] // 2
    rest = jnp.dot(low, weight_ref[:, :half], preferred_element_type=F32)
    return both[:, :half] + both[:, half:] + rest


def fine_rim(source, links_ref, high, low):
    start = device_number() * 4 - 2
    for pair in range(2):
        found = []
        for b in (2 * pair, 2 * pair + 1):
            near = neighbours(links_ref, b, start, 8)
            near[0, 0, 0] = b + 2
            found.append(near)
        for k in range(5):
            for dx in STEPS:
                rows = []
                for near in found:

                    def tile(dy):
                        first = near[dx, dy, -1 if k == 0 else 0]
                        second = near[dx, dy, 1 if k == 4 else 0]
                        a = source[first, (k + 3) % 4, PLANE[dx]]
                        b = source[second, k % 4, PLANE[dx]]
                        return jnp.where(low_lanes(a.shape), a, b)

                    rows.append(shifted_rows(tile))
                for j in range(3):
                    both = jnp.concatenate([rows[0][j], rows[1][j]], axis=1)
                    h, l = split(both)
                    high[j, k, ROOM[dx], 16 * pair : 16 * pair + 16, :] = h
                    low[j, k, ROOM[dx], 16 * pair : 16 * pair + 16, :] = l


def fine_columns(padded, zz):
    return jnp.concatenate(
        [
            padded[j, zz + h, i : i + 8].reshape(256, 128)
            for i in range(3)
            for j in range(3)
            for h in range(2)
        ],
        axis=1,
    )


def fine_in_kernel(
    codes_ref, links_ref, low_ref, own_ref, high_ref, weight_ref, bias_ref,
    hidden_ref, pooled_ref, source, flat, high, low, sums,
):
    source[8] = jnp.zeros((4, 8, 8, 128), F32)
    pieces = [low_ref[...], own_ref[0:2], own_ref[2:4], high_ref[...]]
    for p, piece in enumerate(pieces):
        flat[...] = piece.reshape(128, 512).T
        for zz in range(4):
            odd = flat[pl.ds(2 * zz + 1, 64, 8), :]
            even = flat[pl.ds(2 * zz, 64, 8), :]
            lower = low_lanes(odd.shape)
            source[2 * p, zz] = jnp.where(lower, odd, swap(even)).reshape(8, 8, 128)
            source[2 * p + 1, zz] = jnp.where(lower, swap(odd), even).reshape(8, 8, 128)
    fine_rim(source, links_ref, high, low)
    held = []
    for zz in range(4):
        r = product(fine_columns(high, zz), fine_columns(low, zz), weight_ref) + bias_ref[...]
        r = silu(r).reshape(8, 32, 128)
        for b in range(4):
            hidden_ref[b, zz] = r[:, 8 * b : 8 * b + 8]
        r = r.reshape(4, 2, 32, 128)
        r = r[:, 0] + r[:, 1]
        held.append(r + swap(r))
        if zz % 2 == 1:
            both = jnp.where(low_lanes(r.shape), held[zz - 1], held[zz])
            sums[64 * zz - 64 : 64 * zz + 64, :] = both.reshape(128, 128)
    means = (sums[pl.ds(0, 128, 2), :] + sums[pl.ds(1, 128, 2), :]) * 0.125
    for n in range(8):
        for b in range(4):
            at = (4 * n + b) * 4
            pooled_ref[32 * b + 4 * n : 32 * b + 4 * n + 4, :] = means[at : at + 4]
    lane = lax.broadcasted_iota(jnp.int32, (8, 128), 1)
    named = jnp.zeros((8, 128), F32)
    for b in range(4):
        named = jnp.where(lane == b, codes_ref[b].astype(F32), named)
    pooled_ref[128:136, :] = named


def collect_kernel(all_ref, cubes_ref, codes_ref, held, spelled, place, sem):
    held[...] = all_ref[:, 128, :]
    copy = pltpu.make_async_copy(held, spelled, sem)
    copy.start()
    copy.wait()
    base = lax.axis_index("dev") * 16
    for t in range(16):
        place[t] = -1

    def note(i, carry):
        code = spelled[i // 4, i % 4].astype(jnp.int32)
        codes_ref[i] = code
        local = code - base

        @pl.when((local >= 0) & (local < 16))
        def _():
            place[local] = i

        return carry

    lax.fori_loop(0, 64, note, 0)
    for t in range(16):
        s, a, b, c = t // 8, t // 4 % 2, t // 2 % 2, t % 2
        i = place[t]
        at = jnp.maximum(i, 0)
        v = all_ref[at // 4, pl.ds(pl.multiple_of(at % 4 * 32, 32), 32), :]
        v = jnp.where(i >= 0, v, 0.0)
        for r in range(8):
            cubes_ref[s, a, c, r, 4 * b : 4 * b + 4, :] = v[4 * r : 4 * r + 4]


def coarse_rim(source, links_ref, high, low):
    start = device_number() * 2 - 2
    found = []
    for s in range(2):
        near = neighbours(links_ref, s, start, 6)
        near[0, 0, 0] = s + 2
        found.append(near)
    for z in range(10):
        dz = -1 if z == 0 else 1 if z == 9 else 0
        at = {-1: 7, 0: z - 1, 1: 0}[dz]
        for dx in STEPS:
            rows = [
                shifted_rows(lambda dy, near=near: source[near[dx, dy, dz], at, PLANE[dx]])
                for near in found
            ]
            for j in range(3):
                h, l = split(jnp.concatenate([rows[0][j], rows[1][j]], axis=1))
                high[j, z, ROOM[dx]] = h
                low[j, z, ROOM[dx]] = l


def coarse_columns(padded, z):
    return jnp.concatenate(
        [
            padded[j, z + l : z + l + 2, i : i + 8].reshape(256, 128)
            for i in range(3)
            for j in range(3)
            for l in range(3)
        ],
        axis=1,
    )


def coarse_first_kernel(
    links_ref, low_ref, own_ref, high_ref, down_ref, weight_ref, bias_ref, first_ref, source, high, low
):
    source[6] = jnp.zeros((8, 8, 8, 128), F32)
    for p, part in enumerate((low_ref, own_ref, high_ref)):
        for s in range(2):
            h, l = split(part[s].reshape(256, 128))
            based = product(h, l, down_ref).reshape(2, 2, 2, 4, 8, 256)
            for a in range(2):
                for z in range(8):
                    source[2 * p + s, z, 4 * a : 4 * a + 4] = based[
                        a, z // 4, z // 2 % 2, :, :, 128 * (z % 2) : 128 * (z % 2) + 128
                    ]
    coarse_rim(source, links_ref, high, low)
    for z in range(0, 8, 2):
        r = product(coarse_columns(high, z), coarse_columns(low, z), weight_ref) + bias_ref[...]
        r = silu(r).reshape(2, 8, 16, 128)
        for s in range(2):
            first_ref[s, z : z + 2] = r[:, :, 8 * s : 8 * s + 8]


def coarse_second_kernel(
    links_ref, codes_ref, low_ref, own_ref, high_ref, weight_ref, bias_ref, up_ref,
    out_ref, source, high, low, octants,
):
    source[6] = jnp.zeros((8, 8, 8, 128), F32)
    for p, part in enumerate((low_ref, own_ref, high_ref)):
        source[2 * p : 2 * p + 2] = part[...]
    coarse_rim(source, links_ref, high, low)
    for z in range(0, 8, 2):
        c, q = z // 4, z // 2 % 2
        r = product(coarse_columns(high, z), coarse_columns(low, z), weight_ref) + bias_ref[...]
        r = silu(r)
        h, l = split(jnp.concatenate([r[:128], r[128:]], axis=1))
        lifted = product(h, l, up_ref)
        for t in range(c, 16, 2):
            s, a, b = t // 8, t // 4 % 2, t // 2 % 2
            for x in range(4):
                at = (4 * a + x) * 16 + 8 * s + 4 * b
                octants[t, 16 * q + 4 * x : 16 * q + 4 * x + 4, :] = lifted[at : at + 4]
    base = lax.axis_index("dev") * 16

    def place(i, carry):
        local = codes_ref[i] - base
        known = (local >= 0) & (local < 16)
        v = octants[jnp.clip(local, 0, 15)]
        out_ref[i] = jnp.where(known, v, 0.0)
        return carry

    lax.fori_loop(0, 64, place, 0)


def blend_kernel(hidden_ref, risen_ref, out_ref, grown):
    risen = risen_ref[0]
    for k in range(1, 16):
        risen = risen + risen_ref[k]
    for b in range(4):
        v = risen[32 * b : 32 * b + 32]
        grown[pl.ds(0, 32, 2), :] = v
        grown[pl.ds(1, 32, 2), :] = v
        full = grown[...].reshape(2, 4, 1, 8, 128)
        turned = swap(full)
        lower = low_lanes(full.shape)
        for h in range(2):
            w = jnp.where(lower, full, turned) if h == 0 else jnp.where(lower, turned, full)
            for q in range(2):
                zz = 2 * q + h
                v = silu(hidden_ref[b, zz].reshape(4, 2, 8, 128) + w[q])
                out_ref[b, zz] = v.reshape(8, 8, 128)


def fine_out_kernel(
    links_ref, low_ref, own_ref, high_ref, features_ref, weight_ref, bias_ref, out_ref, source, flat, high, low
):
    source[8] = jnp.zeros((4, 8, 8, 128), F32)
    source[0:2] = low_ref[...]
    source[2:6] = own_ref[...]
    source[6:8] = high_ref[...]
    fine_rim(source, links_ref, high, low)
    for zz in range(4):
        r = product(fine_columns(high, zz), fine_columns(low, zz), weight_ref) + bias_ref[...]
        r = r.reshape(8, 32, 128)
        for p in range(2):
            v0 = r[:, 16 * p : 16 * p + 8].reshape(64, 128)
            v1 = r[:, 16 * p + 8 : 16 * p + 16].reshape(64, 128)
            lower = low_lanes(v0.shape)
            flat[p, pl.ds(2 * zz + 1, 64, 8), :] = jnp.where(lower, v0, swap(v1))
            flat[p, pl.ds(2 * zz, 64, 8), :] = jnp.where(lower, swap(v0), v1)
    for p in range(2):
        out_ref[2 * p : 2 * p + 2] = features_ref[2 * p : 2 * p + 2] + flat[p].T.reshape(2, 64, 512)


def halves(weight):
    high = lax.reduce_precision(weight, exponent_bits=8, mantissa_bits=7)
    return jnp.concatenate([high.astype(BF16), (weight - high).astype(BF16)], axis=1)


def fine_weight(weight):
    taps = weight.reshape(64, 9, 192).transpose(1, 2, 0)
    even = jnp.pad(taps, ((0, 0), (0, 64), (0, 0)))
    odd = jnp.pad(taps, ((0, 0), (64, 0), (0, 0)))
    return halves(jnp.concatenate([odd, even], axis=2).reshape(2304, 128))


def diagonal(weight):
    n, m = weight.shape
    return halves(
        jnp.concatenate(
            [jnp.pad(weight, ((0, n), (0, 0))), jnp.pad(weight, ((n, 0), (0, 0)))], axis=1
        )
    )


def exchanged(first, last):
    count = lax.axis_size(BOTH)
    up = [(i, i + 1) for i in range(count - 1)]
    return lax.ppermute(last, BOTH, up), lax.ppermute(first, BOTH, [(b, a) for a, b in up])


def struct(*shape, dtype=F32):
    return jax.ShapeDtypeStruct(shape, dtype)


def call(kernel, out, scratch, specs, args, flops):
    return pl.pallas_call(
        kernel,
        out_shape=out,
        in_specs=specs,
        out_specs=jax.tree.map(lambda o: SMEM if o.dtype == jnp.int32 else VMEM, out),
        scratch_shapes=scratch,
        cost_estimate=pl.CostEstimate(flops=flops, bytes_accessed=1 << 21, transcendentals=0),
        compiler_params=pltpu.CompilerParams(vmem_limit_bytes=40 << 20),
    )(*args)


def per_device(
    features, fine_links, codes, coarse_links, fine_in_weight, fine_in_bias, down_weight,
    coarse_first_weight, coarse_first_bias, coarse_second_weight, coarse_second_bias,
    up_weight, fine_out_weight, fine_out_bias,
):
    fine_padded = [pltpu.VMEM((3, 5, 10, 32, 128), BF16)] * 2
    coarse_padded = [pltpu.VMEM((3, 10, 10, 16, 128), BF16)] * 2
    fine_source = pltpu.VMEM((9, 4, 8, 8, 128), F32)
    coarse_source = pltpu.VMEM((7, 8, 8, 8, 128), F32)

    below, above = exchanged(features[0:2], features[2:4])
    hidden, pooled = call(
        fine_in_kernel,
        (struct(4, 4, 8, 8, 128), struct(136, 128)),
        [fine_source, pltpu.VMEM((512, 128), F32), *fine_padded, pltpu.VMEM((256, 128), F32)],
        [SMEM, SMEM] + [VMEM] * 5,
        (
            codes, fine_links, below, features, above,
            fine_weight(fine_in_weight), jnp.tile(fine_in_bias, 2)[None],
        ),
        2 * 1024 * 2304 * 384,
    )
    spread = lax.all_to_all(
        jnp.broadcast_to(pooled[None], (16, 136, 128)), "dev", 0, 0, tiled=True
    )
    cubes, group_codes = call(
        collect_kernel,
        (struct(2, 2, 2, 8, 8, 128), struct(64, dtype=jnp.int32)),
        [
            pltpu.VMEM((16, 128), F32), pltpu.SMEM((16, 128), F32),
            pltpu.SMEM((16,), jnp.int32), pltpu.SemaphoreType.DMA,
        ],
        [VMEM],
        (spread,),
        1 << 20,
    )
    below, above = exchanged(cubes, cubes)
    first = call(
        coarse_first_kernel,
        struct(2, 8, 8, 8, 128),
        [coarse_source, *coarse_padded],
        [SMEM] + [VMEM] * 6,
        (
            coarse_links, below, cubes, above, diagonal(down_weight.T),
            halves(coarse_first_weight.T), coarse_first_bias[None],
        ),
        2 * 1024 * 3456 * 384,
    )
    below, above = exchanged(first, first)
    lifted = call(
        coarse_second_kernel,
        struct(64, 32, 128),
        [coarse_source, *coarse_padded, pltpu.VMEM((16, 32, 128), F32)],
        [SMEM, SMEM] + [VMEM] * 6,
        (
            coarse_links, group_codes, below, first, above,
            halves(coarse_second_weight.T), coarse_second_bias[None], diagonal(up_weight.T),
        ),
        2 * 1024 * 3456 * 384,
    )
    risen = lax.all_to_all(lifted.reshape(16, 128, 128), "dev", 0, 0, tiled=True)
    blended = call(
        blend_kernel,
        struct(4, 4, 8, 8, 128),
        [pltpu.VMEM((64, 128), F32)],
        [VMEM, VMEM],
        (hidden, risen),
        1 << 20,
    )
    below, above = exchanged(blended[0:2], blended[2:4])
    return call(
        fine_out_kernel,
        struct(4, 64, 512),
        [fine_source, pltpu.VMEM((2, 512, 128), F32), *fine_padded],
        [SMEM] + [VMEM] * 6,
        (
            fine_links, below, blended, above, features,
            fine_weight(fine_out_weight), jnp.tile(fine_out_bias, 2)[None],
        ),
        2 * 1024 * 2304 * 384,
    )


def solution(mesh):
    split_first = P(BOTH)
    placed = (split_first,) * 4 + (P(),) * 10
    return jax.shard_map(
        per_device,
        mesh=mesh,
        in_specs=placed,
        out_specs=split_first,
        check_vma=False,
    )
```

```python
import jax
import jax.numpy as jnp
from jax import lax
from jax.experimental import pallas as pl
from jax.experimental.pallas import tpu as pltpu
from jax.sharding import PartitionSpec as P

F32, BF16 = jnp.float32, jnp.bfloat16
BOTH = ("grp", "dev")
STEPS = (-1, 0, 1)
COLUMN = {
    offset: k
    for k, offset in enumerate(
        (x, y, z) for x in STEPS for y in STEPS for z in STEPS if (x, y, z) != (0, 0, 0)
    )
}
PLANE = {-1: (56, 8), 0: (0, 64), 1: (0, 8)}
ROOM = {-1: slice(0, 1), 0: slice(1, 9), 1: slice(9, 10)}
VMEM = pl.BlockSpec(memory_space=pltpu.VMEM)
SMEM = pl.BlockSpec(memory_space=pltpu.SMEM)


def silu(v):
    return v / (1.0 + jnp.exp(-v))


def split(v):
    high = v.astype(BF16)
    return high, (v - high.astype(F32)).astype(BF16)


def low_lanes(shape):
    return lax.broadcasted_iota(jnp.int32, shape, len(shape) - 1) < 64


def swap(v):
    return pltpu.roll(v, 64, v.ndim - 1)


def device_number():
    return lax.axis_index("grp") * lax.axis_size("dev") + lax.axis_index("dev")


def neighbours(links_ref, row, start, none):
    found = {}
    for offset, k in COLUMN.items():
        link = links_ref[row, k]
        found[offset] = jnp.where(link < 0, none, link - start)
    return found


def planes(source, brick, z, dx):
    at, count = PLANE[dx]
    return source[brick, 64 * z + at : 64 * z + at + count, :].reshape(count // 8, 8, 128)


def even_device():
    return device_number() % 2 == 0


def fine_pack(brick_ref, n, out_ref, m, middle):
    first, last = brick_ref[n, 0:64], brick_ref[n, 192:256]
    lower = low_lanes(first.shape)
    out_ref[m, 0:64] = jnp.where(lower, last, first)
    middle[0:64] = jnp.where(lower, first, last)
    middle[64:192] = brick_ref[n, 64:192]
    for k in range(3):
        out_ref[m, 64 + 8 * k : 72 + 8 * k] = middle[64 * k : 64 * k + 8]
        out_ref[m, 88 + 8 * k : 96 + 8 * k] = middle[64 * k + 56 : 64 * k + 64]
    out_ref[m, 112:136] = middle[pl.ds(0, 24, 8), :]
    out_ref[m, 136:160] = middle[pl.ds(7, 24, 8), :]


def fine_unpack(packed_ref, m, source, n, middle):
    middle[pl.ds(0, 24, 8), :] = packed_ref[m, 112:136]
    middle[pl.ds(7, 24, 8), :] = packed_ref[m, 136:160]
    for k in range(3):
        middle[64 * k : 64 * k + 8] = packed_ref[m, 64 + 8 * k : 72 + 8 * k]
        middle[64 * k + 56 : 64 * k + 64] = packed_ref[m, 88 + 8 * k : 96 + 8 * k]
    ends, inner = packed_ref[m, 0:64], middle[0:64]
    lower = low_lanes(ends.shape)
    source[n, 0:64] = jnp.where(lower, inner, ends)
    source[n, 64:192] = middle[64:192]
    source[n, 192:256] = jnp.where(lower, ends, inner)


def fine_halo(first_ref, second_ref, source, middle):
    even = even_device()
    for packed_ref, at in ((first_ref, jnp.where(even, 6, 0)), (second_ref, jnp.where(even, 0, 6))):
        for m in range(2):
            fine_unpack(packed_ref, m, source, at + m, middle)


def fine_sends(brick_ref, first_ref, second_ref, middle):
    even = even_device()
    for out_ref, at in ((first_ref, jnp.where(even, 2, 0)), (second_ref, jnp.where(even, 0, 2))):
        for m in range(2):
            fine_pack(brick_ref, at + m, out_ref, m, middle)


def shifted_rows(tile):
    below, here, above = tile(-1), tile(0), tile(1)
    axis = here.ndim - 2
    row = lax.broadcasted_iota(jnp.int32, here.shape, axis)
    return (
        pltpu.roll(jnp.where(row == 7, below, here), 1, axis),
        here,
        pltpu.roll(jnp.where(row == 0, above, here), 7, axis),
    )


def product(high, low, weight_ref):
    both = jnp.dot(high, weight_ref[...], preferred_element_type=F32)
    half = both.shape[1] // 2
    rest = jnp.dot(low, weight_ref[:, :half], preferred_element_type=F32)
    return both[:, :half] + both[:, half:] + rest


def fine_rim(source, links_ref, high, low):
    start = device_number() * 4 - 2
    for pair in range(2):
        found = []
        for b in (2 * pair, 2 * pair + 1):
            near = neighbours(links_ref, b, start, 8)
            near[0, 0, 0] = b + 2
            found.append(near)
        for k in range(5):
            for dx in STEPS:
                rows = []
                for near in found:

                    def tile(dy):
                        first = near[dx, dy, -1 if k == 0 else 0]
                        second = near[dx, dy, 1 if k == 4 else 0]
                        a = planes(source, first, (k + 3) % 4, dx)
                        b = planes(source, second, k % 4, dx)
                        return jnp.where(low_lanes(a.shape), a, b)

                    rows.append(shifted_rows(tile))
                for j in range(3):
                    both = jnp.concatenate([rows[0][j], rows[1][j]], axis=1)
                    h, l = split(both)
                    high[j, k, ROOM[dx], 16 * pair : 16 * pair + 16, :] = h
                    low[j, k, ROOM[dx], 16 * pair : 16 * pair + 16, :] = l


def fine_columns(padded, zz):
    return jnp.concatenate(
        [
            padded[j, zz + h, i : i + 8].reshape(256, 128)
            for i in range(3)
            for j in range(3)
            for h in range(2)
        ],
        axis=1,
    )


def turn_kernel(features_ref, own_ref, first_ref, second_ref, flat, middle):
    for p in range(2):
        flat[...] = features_ref[2 * p : 2 * p + 2].reshape(128, 512).T
        for zz in range(4):
            odd = flat[pl.ds(2 * zz + 1, 64, 8), :]
            even = flat[pl.ds(2 * zz, 64, 8), :]
            lower = low_lanes(odd.shape)
            own_ref[2 * p, 64 * zz : 64 * zz + 64] = jnp.where(lower, odd, swap(even))
            own_ref[2 * p + 1, 64 * zz : 64 * zz + 64] = jnp.where(lower, swap(odd), even)
    fine_sends(own_ref, first_ref, second_ref, middle)


def fine_weight_rows(weight_ref, out_ref):
    taps = []
    for at in range(0, 1728, 128):
        part = weight_ref[:, at : min(at + 128, 1728)]
        turned = jnp.concatenate([part, part], axis=0).T
        taps += [turned[r : r + 64] for r in range(0, turned.shape[0], 64)]
    nothing = jnp.zeros((64, 128), F32)
    lower = low_lanes((64, 128))
    for n in range(9):
        for z in range(4):
            odd = taps[3 * n + z - 1] if z >= 1 else nothing
            even = taps[3 * n + z] if z <= 2 else nothing
            h, l = split(jnp.where(lower, odd, even))
            at = 256 * n + 64 * z
            out_ref[at : at + 64, 0:128] = h
            out_ref[at : at + 64, 128:256] = l


def coarse_weight_rows(weight_ref, out_ref):
    for at in range(0, 3456, 128):
        h, l = split(weight_ref[:, at : at + 128].T)
        out_ref[at : at + 128, 0:128] = h
        out_ref[at : at + 128, 128:256] = l


def first_weight_kernel(weight_ref, out_ref):
    fine_weight_rows(weight_ref, out_ref)


def later_weights_kernel(
    first_ref, second_ref, down_ref, up_ref, fine_ref, first_out, second_out, down_out, up_out, fine_out
):
    coarse_weight_rows(first_ref, first_out)
    coarse_weight_rows(second_ref, second_out)
    fine_weight_rows(fine_ref, fine_out)
    nothing = jnp.zeros((64, 128), F32)
    h, l = split(jnp.concatenate([down_ref[...].T, nothing], axis=0))
    down_out[:, 0:128] = h
    down_out[:, 256:384] = l
    h, l = split(jnp.concatenate([nothing, down_ref[...].T], axis=0))
    down_out[:, 128:256] = h
    down_out[:, 384:512] = l
    both = jnp.concatenate([up_ref[...], up_ref[...]], axis=0).T
    lower = low_lanes(both.shape)
    for k in range(2):
        h, l = split(jnp.where(lower if k == 0 else ~lower, both, 0.0))
        up_out[128 * k : 128 * k + 128, 0:128] = h
        up_out[128 * k : 128 * k + 128, 128:256] = l


def fine_in_kernel(
    codes_ref, links_ref, own_ref, first_ref, second_ref, weight_ref, bias_ref,
    hidden_ref, pooled_ref, source, high, low, sums, middle,
):
    source[8] = jnp.zeros((256, 128), F32)
    source[2:6] = own_ref[...]
    fine_halo(first_ref, second_ref, source, middle)
    fine_rim(source, links_ref, high, low)
    bias = jnp.concatenate([bias_ref[...]] * 2, axis=1)
    held = []
    for zz in range(4):
        r = product(fine_columns(high, zz), fine_columns(low, zz), weight_ref) + bias
        r = silu(r).reshape(8, 32, 128)
        for b in range(4):
            hidden_ref[b, 64 * zz : 64 * zz + 64] = r[:, 8 * b : 8 * b + 8].reshape(64, 128)
        r = r.reshape(4, 2, 32, 128)
        r = r[:, 0] + r[:, 1]
        held.append(r + swap(r))
        if zz % 2 == 1:
            both = jnp.where(low_lanes(r.shape), held[zz - 1], held[zz])
            sums[64 * zz - 64 : 64 * zz + 64, :] = both.reshape(128, 128)
    means = (sums[pl.ds(0, 128, 2), :] + sums[pl.ds(1, 128, 2), :]) * 0.125
    for n in range(8):
        for b in range(4):
            at = (4 * n + b) * 4
            pooled_ref[0, 32 * b + 4 * n : 32 * b + 4 * n + 4, :] = means[at : at + 4]
    lane = lax.broadcasted_iota(jnp.int32, (8, 128), 1)
    named = jnp.zeros((8, 128), F32)
    for b in range(4):
        named = jnp.where(lane == b, codes_ref[b].astype(F32), named)
    pooled_ref[0, 128:136, :] = named
    for k in range(1, 16):
        pooled_ref[k] = pooled_ref[0]


def cube_rows(all_ref, place_ref, code, store):
    for t in range(16):
        a, b, c = t // 4 % 2, t // 2 % 2, t % 2
        i = place_ref[code + t]
        at = jnp.maximum(i, 0)
        v = all_ref[at // 4, pl.ds(pl.multiple_of(at % 4 * 32, 32), 32), :]
        v = jnp.where(i >= 0, v, 0.0)
        for r in range(8):
            store(t // 8, ((2 * a + c) * 8 + r) * 8 + 4 * b, v[4 * r : 4 * r + 4])


def edge_kernel(all_ref, cubes_ref, place_ref, codes_ref, held, spelled, sem):
    held[...] = all_ref[:, 128, :]
    copy = pltpu.make_async_copy(held, spelled, sem)
    copy.start()
    me = lax.axis_index("dev")
    for t in range(256):
        place_ref[t] = -1
    copy.wait()
    for i in range(64):
        code = spelled[i // 4, i % 4].astype(jnp.int32)
        codes_ref[i] = code
        place_ref[code] = i

    @pl.when((me == 0) | (me == 15))
    def _():
        def store(s, at, v):
            cubes_ref[s, at : at + 4, :] = v

        cube_rows(all_ref, place_ref, jnp.where(me == 0, 15 * 16, 0), store)


def bring_down(cubes, down_ref, source, n):
    h, l = split(cubes)
    based = product(h, l, down_ref).reshape(2, 2, 2, 32, 256)
    for a in range(2):
        for z in range(8):
            source[n, 64 * z + 32 * a : 64 * z + 32 * a + 32] = based[
                a, z // 4, z // 2 % 2, :, 128 * (z % 2) : 128 * (z % 2) + 128
            ]


def base_kernel(all_ref, place_ref, down_ref, out_ref, cubes):
    me = lax.axis_index("dev")
    for n in range(3):
        owner = jnp.clip(me + (n - 1), 0, 15)

        def store(s, at, v):
            cubes[s, at : at + 4, :] = v

        cube_rows(all_ref, place_ref, owner * 16, store)
        for s in range(2):
            bring_down(cubes[s], down_ref, out_ref, 2 * n + s)


def coarse_rim(source, links_ref, high, low):
    start = device_number() * 2 - 2
    found = []
    for s in range(2):
        near = neighbours(links_ref, s, start, 6)
        near[0, 0, 0] = s + 2
        found.append(near)
    for z in range(10):
        dz = -1 if z == 0 else 1 if z == 9 else 0
        at = {-1: 7, 0: z - 1, 1: 0}[dz]
        for dx in STEPS:
            rows = [
                shifted_rows(lambda dy, near=near: planes(source, near[dx, dy, dz], at, dx))
                for near in found
            ]
            for j in range(3):
                h, l = split(jnp.concatenate([rows[0][j], rows[1][j]], axis=1))
                high[j, z, ROOM[dx]] = h
                low[j, z, ROOM[dx]] = l


def coarse_columns(padded, z):
    return jnp.concatenate(
        [
            padded[j, z + l : z + l + 2, i : i + 8].reshape(256, 128)
            for i in range(3)
            for j in range(3)
            for l in range(3)
        ],
        axis=1,
    )


def coarse_first_kernel(
    links_ref, based_ref, edge_ref, down_ref, weight_ref, bias_ref, first_ref, packed_ref, source, high, low
):
    source[6] = jnp.zeros((512, 128), F32)
    source[0:6] = based_ref[...]
    me = lax.axis_index("dev")

    @pl.when((me == 0) | (me == 15))
    def _():
        at = jnp.where(me == 0, 0, 4)
        for s in range(2):
            bring_down(edge_ref[s], down_ref, source, at + s)

    coarse_rim(source, links_ref, high, low)
    for z in range(0, 8, 2):
        r = product(coarse_columns(high, z), coarse_columns(low, z), weight_ref) + bias_ref[...]
        r = silu(r).reshape(2, 8, 16, 128)
        for s in range(2):
            first_ref[s, 64 * z : 64 * z + 128] = r[:, :, 8 * s : 8 * s + 8].reshape(128, 128)
    for s in range(2):
        packed_ref[s, 0:64] = first_ref[s, 0:64]
        packed_ref[s, 64:128] = first_ref[s, 448:512]
        for z in range(1, 7):
            packed_ref[s, 120 + 8 * z : 128 + 8 * z] = first_ref[s, 64 * z : 64 * z + 8]
            packed_ref[s, 168 + 8 * z : 176 + 8 * z] = first_ref[s, 64 * z + 56 : 64 * z + 64]
        packed_ref[s, 224:272] = first_ref[s, pl.ds(64, 48, 8), :]
        packed_ref[s, 272:320] = first_ref[s, pl.ds(71, 48, 8), :]


def coarse_second_kernel(
    links_ref, codes_ref, own_ref, first_ref, second_ref, weight_ref, bias_ref, up_ref,
    out_ref, source, high, low, octants,
):
    source[6] = jnp.zeros((512, 128), F32)
    source[2:4] = own_ref[...]
    even = even_device()
    for packed_ref, n in ((first_ref, jnp.where(even, 4, 0)), (second_ref, jnp.where(even, 0, 4))):
        for s in range(2):
            source[n + s, pl.ds(64, 48, 8), :] = packed_ref[s, 224:272]
            source[n + s, pl.ds(71, 48, 8), :] = packed_ref[s, 272:320]
            source[n + s, 0:64] = packed_ref[s, 0:64]
            source[n + s, 448:512] = packed_ref[s, 64:128]
            for z in range(1, 7):
                source[n + s, 64 * z : 64 * z + 8] = packed_ref[s, 120 + 8 * z : 128 + 8 * z]
                source[n + s, 64 * z + 56 : 64 * z + 64] = packed_ref[s, 168 + 8 * z : 176 + 8 * z]
    coarse_rim(source, links_ref, high, low)
    for z in range(0, 8, 2):
        c, q = z // 4, z // 2 % 2
        r = product(coarse_columns(high, z), coarse_columns(low, z), weight_ref) + bias_ref[...]
        r = silu(r)
        h, l = split(jnp.concatenate([r[:128], r[128:]], axis=1))
        lifted = product(h, l, up_ref)
        for t in range(c, 16, 2):
            s, a, b = t // 8, t // 4 % 2, t // 2 % 2
            for x in range(4):
                at = (4 * a + x) * 16 + 8 * s + 4 * b
                octants[t, 16 * q + 4 * x : 16 * q + 4 * x + 4, :] = lifted[at : at + 4]
    base = lax.axis_index("dev") * 16

    def place(i, carry):
        local = codes_ref[i] - base
        known = (local >= 0) & (local < 16)
        v = octants[jnp.clip(local, 0, 15)]
        out_ref[i] = jnp.where(known, v, 0.0)
        return carry

    lax.fori_loop(0, 64, place, 0)


def blend_kernel(hidden_ref, risen_ref, out_ref, first_ref, second_ref, grown, middle):
    risen = risen_ref[0]
    for k in range(1, 16):
        risen = risen + risen_ref[k]
    for b in range(4):
        v = risen[32 * b : 32 * b + 32]
        grown[pl.ds(0, 32, 2), :] = v
        grown[pl.ds(1, 32, 2), :] = v
        full = grown[...].reshape(2, 4, 1, 8, 128)
        turned = swap(full)
        lower = low_lanes(full.shape)
        for h in range(2):
            w = jnp.where(lower, full, turned) if h == 0 else jnp.where(lower, turned, full)
            for q in range(2):
                at = 64 * (2 * q + h)
                v = silu(hidden_ref[b, at : at + 64].reshape(4, 2, 8, 128) + w[q])
                out_ref[b, at : at + 64] = v.reshape(64, 128)
    fine_sends(out_ref, first_ref, second_ref, middle)


def fine_out_kernel(
    links_ref, own_ref, first_ref, second_ref, features_ref, weight_ref, bias_ref,
    out_ref, source, flat, high, low, middle,
):
    source[8] = jnp.zeros((256, 128), F32)
    source[2:6] = own_ref[...]
    fine_halo(first_ref, second_ref, source, middle)
    fine_rim(source, links_ref, high, low)
    bias = jnp.concatenate([bias_ref[...]] * 2, axis=1)
    for zz in range(4):
        r = product(fine_columns(high, zz), fine_columns(low, zz), weight_ref) + bias
        r = r.reshape(8, 32, 128)
        for p in range(2):
            v0 = r[:, 16 * p : 16 * p + 8].reshape(64, 128)
            v1 = r[:, 16 * p + 8 : 16 * p + 16].reshape(64, 128)
            lower = low_lanes(v0.shape)
            flat[p, pl.ds(2 * zz + 1, 64, 8), :] = jnp.where(lower, v0, swap(v1))
            flat[p, pl.ds(2 * zz, 64, 8), :] = jnp.where(lower, swap(v0), v1)
    for p in range(2):
        out_ref[2 * p : 2 * p + 2] = features_ref[2 * p : 2 * p + 2] + flat[p].T.reshape(2, 64, 512)


def exchanged(first, second):
    count = lax.axis_size(BOTH)
    inner = [(i, i ^ 1) for i in range(count)]
    outer = [(i, i + 1) for i in range(1, count - 1, 2)]
    outer += [(b, a) for a, b in outer]
    return lax.ppermute(first, BOTH, inner), lax.ppermute(second, BOTH, outer)


def struct(*shape, dtype=F32):
    return jax.ShapeDtypeStruct(shape, dtype)


def call(kernel, out, scratch, specs, args, flops):
    return pl.pallas_call(
        kernel,
        out_shape=out,
        in_specs=specs,
        out_specs=jax.tree.map(lambda o: SMEM if o.dtype == jnp.int32 else VMEM, out),
        scratch_shapes=scratch,
        cost_estimate=pl.CostEstimate(flops=flops, bytes_accessed=1 << 21, transcendentals=0),
        compiler_params=pltpu.CompilerParams(vmem_limit_bytes=40 << 20),
    )(*args)


def per_device(
    features, fine_links, codes, coarse_links, fine_in_weight, fine_in_bias, down_weight,
    coarse_first_weight, coarse_first_bias, coarse_second_weight, coarse_second_bias,
    up_weight, fine_out_weight, fine_out_bias,
):
    fine_padded = [pltpu.VMEM((3, 5, 10, 32, 128), BF16)] * 2
    coarse_padded = [pltpu.VMEM((3, 10, 10, 16, 128), BF16)] * 2
    fine_source = pltpu.VMEM((9, 256, 128), F32)
    coarse_source = pltpu.VMEM((7, 512, 128), F32)
    middle = pltpu.VMEM((192, 128), F32)
    brick, shell = struct(4, 256, 128), struct(2, 160, 128)

    own, first, second = call(
        turn_kernel,
        (brick, shell, shell),
        [pltpu.VMEM((512, 128), F32), middle],
        [VMEM],
        (features,),
        1 << 20,
    )
    first, second = exchanged(first, second)
    weight_in = call(
        first_weight_kernel, struct(2304, 256, dtype=BF16), [], [VMEM], (fine_in_weight,), 1 << 20
    )
    hidden, pooled = call(
        fine_in_kernel,
        (brick, struct(16, 136, 128)),
        [fine_source, *fine_padded, pltpu.VMEM((256, 128), F32), middle],
        [SMEM, SMEM] + [VMEM] * 5,
        (codes, fine_links, own, first, second, weight_in, fine_in_bias[None]),
        2 * 1024 * 2304 * 384,
    )
    later = (coarse_first_weight, coarse_second_weight, down_weight, up_weight, fine_out_weight)
    pooled, *later = lax.optimization_barrier((pooled, *later))
    weight_first, weight_second, down, up, weight_out = call(
        later_weights_kernel,
        (
            struct(3456, 256, dtype=BF16), struct(3456, 256, dtype=BF16),
            struct(128, 512, dtype=BF16), struct(256, 256, dtype=BF16),
            struct(2304, 256, dtype=BF16),
        ),
        [],
        [VMEM] * 5,
        later,
        1 << 30,
    )
    spread = lax.all_to_all(pooled, "dev", 0, 0, tiled=True)
    cubes, place, group_codes = call(
        edge_kernel,
        (struct(2, 256, 128), struct(256, dtype=jnp.int32), struct(64, dtype=jnp.int32)),
        [pltpu.VMEM((16, 128), F32), pltpu.SMEM((16, 128), F32), pltpu.SemaphoreType.DMA],
        [VMEM],
        (spread,),
        1 << 20,
    )
    groups, devices = lax.axis_size("grp"), lax.axis_size("dev")
    edges = [(g * devices, (g + 1) * devices) for g in range(groups - 1)]
    edges += [((g + 2) * devices - 1, (g + 1) * devices - 1) for g in range(groups - 1)]
    edge = lax.ppermute(cubes, BOTH, edges)
    based = call(
        base_kernel,
        struct(6, 512, 128),
        [pltpu.VMEM((2, 256, 128), F32)],
        [VMEM, SMEM, VMEM],
        (spread, place, down),
        1 << 28,
    )
    first_own, packed = call(
        coarse_first_kernel,
        (struct(2, 512, 128), struct(2, 320, 128)),
        [coarse_source, *coarse_padded],
        [SMEM] + [VMEM] * 5,
        (coarse_links, based, edge, down, weight_first, coarse_first_bias[None]),
        2 * 1024 * 3456 * 384,
    )
    first, second = exchanged(packed, packed)
    lifted = call(
        coarse_second_kernel,
        struct(64, 32, 128),
        [coarse_source, *coarse_padded, pltpu.VMEM((16, 32, 128), F32)],
        [SMEM, SMEM] + [VMEM] * 6,
        (
            coarse_links, group_codes, first_own, first, second, weight_second,
            coarse_second_bias[None], up,
        ),
        2 * 1024 * 3456 * 384,
    )
    risen = lax.all_to_all(lifted.reshape(16, 128, 128), "dev", 0, 0, tiled=True)
    blended, first, second = call(
        blend_kernel,
        (brick, shell, shell),
        [pltpu.VMEM((64, 128), F32), middle],
        [VMEM, VMEM],
        (hidden, risen),
        1 << 20,
    )
    first, second = exchanged(first, second)
    return call(
        fine_out_kernel,
        struct(4, 64, 512),
        [fine_source, pltpu.VMEM((2, 512, 128), F32), *fine_padded, middle],
        [SMEM] + [VMEM] * 6,
        (fine_links, blended, first, second, features, weight_out, fine_out_bias[None]),
        2 * 1024 * 2304 * 384,
    )


def solution(mesh):
    split_first = P(BOTH)
    placed = (split_first,) * 4 + (P(),) * 10
    return jax.shard_map(
        per_device,
        mesh=mesh,
        in_specs=placed,
        out_specs=split_first,
        check_vma=False,
    )
```

```python
import jax
import jax.numpy as jnp
from jax import lax
from jax.experimental import pallas as pl
from jax.experimental.pallas import tpu as pltpu
from jax.sharding import PartitionSpec as P

F32, BF16 = jnp.float32, jnp.bfloat16
BOTH = ("grp", "dev")
STEPS = (-1, 0, 1)
COLUMN = {
    offset: k
    for k, offset in enumerate(
        (x, y, z) for x in STEPS for y in STEPS for z in STEPS if (x, y, z) != (0, 0, 0)
    )
}
PLANE = {-1: (56, 8), 0: (0, 64), 1: (0, 8)}
ROOM = {-1: slice(0, 1), 0: slice(1, 9), 1: slice(9, 10)}
VMEM = pl.BlockSpec(memory_space=pltpu.VMEM)
SMEM = pl.BlockSpec(memory_space=pltpu.SMEM)


def silu(v):
    return v / (1.0 + jnp.exp(-v))


def split(v):
    high = v.astype(BF16)
    return high, (v - high.astype(F32)).astype(BF16)


def low_lanes(shape):
    return lax.broadcasted_iota(jnp.int32, shape, len(shape) - 1) < 64


def swap(v):
    return pltpu.roll(v, 64, v.ndim - 1)


def device_number():
    return lax.axis_index("grp") * lax.axis_size("dev") + lax.axis_index("dev")


def neighbours(links_ref, row, start, none):
    found = {}
    for offset, k in COLUMN.items():
        link = links_ref[row, k].astype(jnp.int32)
        found[offset] = jnp.where(link < 0, none, jnp.clip(link - start, 0, none))
    return found


def planes(source, brick, z, dx):
    at, count = PLANE[dx]
    return source[brick, 64 * z + at : 64 * z + at + count, :].reshape(count // 8, 8, 128)


def even_device():
    return device_number() % 2 == 0


def fine_pack(brick_ref, out_ref, middle):
    first, last = brick_ref[0:64], brick_ref[192:256]
    lower = low_lanes(first.shape)
    out_ref[0:64] = jnp.where(lower, last, first)
    middle[0:64] = jnp.where(lower, first, last)
    middle[64:192] = brick_ref[64:192]
    for k in range(3):
        out_ref[64 + 8 * k : 72 + 8 * k] = middle[64 * k : 64 * k + 8]
        out_ref[88 + 8 * k : 96 + 8 * k] = middle[64 * k + 56 : 64 * k + 64]
    out_ref[112:136] = middle[pl.ds(0, 24, 8), :]
    out_ref[136:160] = middle[pl.ds(7, 24, 8), :]


def fine_unpack(packed_ref, brick_ref, middle):
    middle[pl.ds(0, 24, 8), :] = packed_ref[112:136]
    middle[pl.ds(7, 24, 8), :] = packed_ref[136:160]
    for k in range(3):
        middle[64 * k : 64 * k + 8] = packed_ref[64 + 8 * k : 72 + 8 * k]
        middle[64 * k + 56 : 64 * k + 64] = packed_ref[88 + 8 * k : 96 + 8 * k]
    ends, inner = packed_ref[0:64], middle[0:64]
    lower = low_lanes(ends.shape)
    brick_ref[0:64] = jnp.where(lower, inner, ends)
    brick_ref[64:192] = middle[64:192]
    brick_ref[192:256] = jnp.where(lower, ends, inner)


def fine_halo(first_ref, second_ref, source, middle):
    even = even_device()
    for packed_ref, at in ((first_ref, jnp.where(even, 6, 0)), (second_ref, jnp.where(even, 0, 6))):
        for m in range(2):
            fine_unpack(packed_ref.at[m], source.at[at + m], middle)


def fine_sends(brick_ref, first_ref, second_ref, middle):
    even = even_device()
    for out_ref, at in ((first_ref, jnp.where(even, 2, 0)), (second_ref, jnp.where(even, 0, 2))):
        for m in range(2):
            fine_pack(brick_ref.at[at + m], out_ref.at[m], middle)


def shifted_rows(tile):
    below, here, above = tile(-1), tile(0), tile(1)
    axis = here.ndim - 2
    row = lax.broadcasted_iota(jnp.int32, here.shape, axis)
    return (
        pltpu.roll(jnp.where(row == 7, below, here), 1, axis),
        here,
        pltpu.roll(jnp.where(row == 0, above, here), 7, axis),
    )


def product(high, low, weight_ref):
    both = jnp.dot(high, weight_ref[...], preferred_element_type=F32)
    half = both.shape[1] // 2
    rest = jnp.dot(low, weight_ref[:, :half], preferred_element_type=F32)
    return both[:, :half] + both[:, half:] + rest


def fine_rim(source, links_ref, high, low):
    start = device_number() * 4 - 2
    for pair in range(2):
        found = []
        for b in (2 * pair, 2 * pair + 1):
            near = neighbours(links_ref, b, start, 8)
            near[0, 0, 0] = b + 2
            found.append(near)
        for k in range(5):
            for dx in STEPS:
                rows = []
                for near in found:

                    def tile(dy):
                        first = near[dx, dy, -1 if k == 0 else 0]
                        second = near[dx, dy, 1 if k == 4 else 0]
                        a = planes(source, first, (k + 3) % 4, dx)
                        b = planes(source, second, k % 4, dx)
                        return jnp.where(low_lanes(a.shape), a, b)

                    rows.append(shifted_rows(tile))
                for j in range(3):
                    both = jnp.concatenate([rows[0][j], rows[1][j]], axis=1)
                    h, l = split(both)
                    high[j, k, ROOM[dx], 16 * pair : 16 * pair + 16, :] = h
                    low[j, k, ROOM[dx], 16 * pair : 16 * pair + 16, :] = l


def fine_columns(padded, zz):
    return jnp.concatenate(
        [
            padded[j, zz + h, i : i + 8].reshape(256, 128)
            for i in range(3)
            for j in range(3)
            for h in range(2)
        ],
        axis=1,
    )


def turn_kernel(features_ref, own_ref, first_ref, second_ref, flat, middle):
    for p in range(2):
        flat[...] = features_ref[2 * p : 2 * p + 2].reshape(128, 512).T
        for zz in range(4):
            odd = flat[pl.ds(2 * zz + 1, 64, 8), :]
            even = flat[pl.ds(2 * zz, 64, 8), :]
            lower = low_lanes(odd.shape)
            own_ref[2 * p, 64 * zz : 64 * zz + 64] = jnp.where(lower, odd, swap(even))
            own_ref[2 * p + 1, 64 * zz : 64 * zz + 64] = jnp.where(lower, swap(odd), even)
    fine_sends(own_ref, first_ref, second_ref, middle)


def fine_weight_rows(weight_ref, out_ref):
    taps = []
    for at in range(0, 1728, 128):
        part = weight_ref[:, at : min(at + 128, 1728)]
        turned = jnp.concatenate([part, part], axis=0).T
        taps += [turned[r : r + 64] for r in range(0, turned.shape[0], 64)]
    nothing = jnp.zeros((64, 128), F32)
    lower = low_lanes((64, 128))
    for n in range(9):
        for z in range(4):
            odd = taps[3 * n + z - 1] if z >= 1 else nothing
            even = taps[3 * n + z] if z <= 2 else nothing
            h, l = split(jnp.where(lower, odd, even))
            at = 256 * n + 64 * z
            out_ref[at : at + 64, 0:128] = h
            out_ref[at : at + 64, 128:256] = l


def coarse_weight_rows(weight_ref, out_ref):
    for at in range(0, 3456, 128):
        h, l = split(weight_ref[:, at : at + 128].T)
        out_ref[at : at + 128, 0:128] = h
        out_ref[at : at + 128, 128:256] = l


def first_weight_kernel(weight_ref, out_ref):
    fine_weight_rows(weight_ref, out_ref)


def later_weights_kernel(
    first_ref, second_ref, down_ref, up_ref, fine_ref, first_out, second_out, down_out, up_out, fine_out
):
    coarse_weight_rows(first_ref, first_out)
    coarse_weight_rows(second_ref, second_out)
    fine_weight_rows(fine_ref, fine_out)
    nothing = jnp.zeros((64, 128), F32)
    h, l = split(jnp.concatenate([down_ref[...].T, nothing], axis=0))
    down_out[:, 0:128] = h
    down_out[:, 256:384] = l
    h, l = split(jnp.concatenate([nothing, down_ref[...].T], axis=0))
    down_out[:, 128:256] = h
    down_out[:, 384:512] = l
    both = jnp.concatenate([up_ref[...], up_ref[...]], axis=0).T
    lower = low_lanes(both.shape)
    for k in range(2):
        h, l = split(jnp.where(lower if k == 0 else ~lower, both, 0.0))
        up_out[128 * k : 128 * k + 128, 0:128] = h
        up_out[128 * k : 128 * k + 128, 128:256] = l


def fine_in_kernel(
    codes_ref, links_ref, coarse_links_ref, own_ref, first_ref, second_ref, weight_ref, bias_ref,
    hidden_ref, pooled_ref, source, high, low, sums, middle,
):
    source[8] = jnp.zeros((256, 128), F32)
    source[2:6] = own_ref[...]
    fine_halo(first_ref, second_ref, source, middle)
    fine_rim(source, links_ref, high, low)
    bias = jnp.concatenate([bias_ref[...]] * 2, axis=1)
    held = []
    for zz in range(4):
        r = product(fine_columns(high, zz), fine_columns(low, zz), weight_ref) + bias
        r = silu(r).reshape(8, 32, 128)
        for b in range(4):
            hidden_ref[b, 64 * zz : 64 * zz + 64] = r[:, 8 * b : 8 * b + 8].reshape(64, 128)
        r = r.reshape(4, 2, 32, 128)
        r = r[:, 0] + r[:, 1]
        held.append(r + swap(r))
        if zz % 2 == 1:
            both = jnp.where(low_lanes(r.shape), held[zz], held[zz - 1])
            sums[64 * zz - 64 : 64 * zz + 64, :] = both.reshape(128, 128)
    means = (sums[pl.ds(0, 128, 2), :] + sums[pl.ds(1, 128, 2), :]) * 0.125
    for n in range(8):
        for b in range(4):
            at = (4 * n + b) * 4
            pooled_ref[0, 32 * b + 4 * n : 32 * b + 4 * n + 4, :] = means[at : at + 4]
    lane = lax.broadcasted_iota(jnp.int32, (8, 128), 1)
    named = jnp.zeros((8, 128), F32)
    for b in range(4):
        named = jnp.where(lane == b, codes_ref[b].astype(F32), named)
    pooled_ref[0, 128:136, :] = named
    pooled_ref[0, 129:131, 0:26] = coarse_links_ref[...].astype(F32)
    for k in range(1, 16):
        pooled_ref[k] = pooled_ref[0]


def cube_rows(all_ref, place_ref, code, store):
    for t in range(16):
        a, b, c = t // 4 % 2, t // 2 % 2, t % 2
        i = place_ref[code + t]
        at = jnp.maximum(i, 0)
        v = all_ref[at // 4, pl.ds(pl.multiple_of(at % 4 * 32, 32), 32), :]
        v = jnp.where(i >= 0, v, 0.0)
        for r in range(8):
            store(t // 8, (2 * c + r // 4) * 64 + (4 * a + r % 4) * 8 + 4 * b, v[4 * r : 4 * r + 4])


def edge_kernel(all_ref, cubes_ref, place_ref, codes_ref, held, spelled, cubes, middle, sem):
    held[...] = all_ref[:, 128, :]
    copy = pltpu.make_async_copy(held, spelled, sem)
    copy.start()
    me = lax.axis_index("dev")
    for t in range(256):
        place_ref[t] = -1
    copy.wait()
    for i in range(64):
        code = spelled[i // 4, i % 4].astype(jnp.int32)
        codes_ref[i] = code
        place_ref[code] = i
    cubes_ref[832:840] = all_ref[jnp.where(me < 8, 15, 0), 128:136, :]

    @pl.when((me < 2) | (me > 13))
    def _():
        def store(s, at, v):
            cubes_ref[256 * s + at : 256 * s + at + 4, :] = v

        cube_rows(all_ref, place_ref, jnp.where(me < 2, 15, 0) * 16, store)

        def hold(s, at, v):
            cubes[s, at : at + 4, :] = v

        cube_rows(all_ref, place_ref, jnp.where(me < 2, 14, 1) * 16, hold)
        for s in range(2):
            fine_pack(cubes.at[s], cubes_ref.at[512 + 160 * s : 672 + 160 * s], middle)


def bring_down(cubes, down_ref, source, n):
    h, l = split(cubes)
    based = product(h, l, down_ref)
    for z in range(8):
        k = 1 - z % 2
        source[n, 64 * z : 64 * z + 64] = based[64 * (z // 2) : 64 * (z // 2) + 64, 128 * k : 128 * k + 128]


def base_kernel(all_ref, place_ref, down_ref, out_ref, links_ref, cubes):
    me = lax.axis_index("dev")
    links_ref[...] = jnp.zeros((8, 128), F32)
    out_ref[10] = jnp.zeros((512, 128), F32)
    for n in range(5):
        owner = jnp.clip(me + (n - 2), 0, 15)

        def store(s, at, v):
            cubes[s, at : at + 4, :] = v

        cube_rows(all_ref, place_ref, owner * 16, store)
        for s in range(2):
            bring_down(cubes[s], down_ref, out_ref, 2 * n + s)
        if 1 <= n <= 3:
            links_ref[2 * n - 2 : 2 * n] = all_ref[owner, 129:131, :]


def coarse_rim(source, links_ref, row, home, start, none, high, low):
    found = []
    for s in range(2):
        near = neighbours(links_ref, row + s, start, none)
        near[0, 0, 0] = home + s
        found.append(near)
    for z in range(10):
        dz = -1 if z == 0 else 1 if z == 9 else 0
        at = {-1: 7, 0: z - 1, 1: 0}[dz]
        for dx in STEPS:
            rows = [
                shifted_rows(lambda dy, near=near: planes(source, near[dx, dy, dz], at, dx))
                for near in found
            ]
            for j in range(3):
                h, l = split(jnp.concatenate([rows[0][j], rows[1][j]], axis=1))
                high[j, z, ROOM[dx]] = h
                low[j, z, ROOM[dx]] = l


def coarse_columns(padded, z):
    return jnp.concatenate(
        [
            padded[j, z + l : z + l + 2, i : i + 8].reshape(256, 128)
            for i in range(3)
            for j in range(3)
            for l in range(3)
        ],
        axis=1,
    )


def coarse_first_pair(source, links_ref, pair, weight_ref, bias_ref, out_ref, n, high, low):
    coarse_rim(source, links_ref, 2 * pair, 2 * pair + 2, device_number() * 2 - 4, 10, high, low)
    for z in range(0, 8, 2):
        r = product(coarse_columns(high, z), coarse_columns(low, z), weight_ref) + bias_ref[...]
        r = silu(r).reshape(2, 8, 16, 128)
        for s in range(2):
            out_ref[n + s, 64 * z : 64 * z + 128] = r[:, :, 8 * s : 8 * s + 8].reshape(128, 128)


def inner_pair():
    return jnp.where(lax.axis_index("dev") < 8, 2, 0)


def inner_kernel(links_ref, based_ref, weight_ref, bias_ref, out_ref, high, low):
    coarse_first_pair(based_ref, links_ref, inner_pair(), weight_ref, bias_ref, out_ref, 0, high, low)


def coarse_kernel(
    links_ref, near_links_ref, codes_ref, based_ref, edge_ref, inner_ref, down_ref, first_weight_ref, first_bias_ref,
    weight_ref, bias_ref, up_ref, out_ref, source, high, low, seconds, high2, low2, octants, held, spelled,
    cubes, middle, sem,
):
    me = lax.axis_index("dev")
    held[...] = near_links_ref[...]

    @pl.when(me == 0)
    def _():
        held[0:2] = edge_ref[833:835]

    @pl.when(me == 15)
    def _():
        held[4:6] = edge_ref[833:835]

    copy = pltpu.make_async_copy(held, spelled, sem)
    copy.start()
    source[...] = based_ref[...]

    @pl.when((me < 2) | (me > 13))
    def _():
        at = jnp.where(me < 2, jnp.where(me == 0, 2, 0), jnp.where(me == 15, 6, 8))
        for s in range(2):
            bring_down(edge_ref[256 * s : 256 * s + 256], down_ref, source, at + s)

    @pl.when((me == 0) | (me == 15))
    def _():
        at = jnp.where(me == 0, 0, 8)
        for s in range(2):
            fine_unpack(edge_ref.at[512 + 160 * s : 672 + 160 * s], cubes, middle)
            bring_down(cubes[...], down_ref, source, at + s)

    seconds[6] = jnp.zeros((512, 128), F32)
    inner = inner_pair()
    for s in range(2):
        seconds[2 * inner + s] = inner_ref[s]
    copy.wait()
    outer = 2 - inner
    coarse_first_pair(source, spelled, outer, first_weight_ref, first_bias_ref, seconds, 2 * outer, high, low)
    coarse_first_pair(source, spelled, 1, first_weight_ref, first_bias_ref, seconds, 2, high2, low2)
    coarse_rim(seconds, links_ref, 0, 2, device_number() * 2 - 2, 6, high, low)
    for z in range(0, 8, 2):
        c, q = z // 4, z // 2 % 2
        r = product(coarse_columns(high, z), coarse_columns(low, z), weight_ref) + bias_ref[...]
        r = silu(r)
        h, l = split(jnp.concatenate([r[:128], r[128:]], axis=1))
        lifted = product(h, l, up_ref)
        for t in range(c, 16, 2):
            s, a, b = t // 8, t // 4 % 2, t // 2 % 2
            for x in range(4):
                at = (4 * a + x) * 16 + 8 * s + 4 * b
                octants[t, 16 * q + 4 * x : 16 * q + 4 * x + 4, :] = lifted[at : at + 4]
    base = lax.axis_index("dev") * 16

    def place(i, carry):
        local = codes_ref[i] - base
        known = (local >= 0) & (local < 16)
        v = octants[jnp.clip(local, 0, 15)]
        out_ref[i] = jnp.where(known, v, 0.0)
        return carry

    lax.fori_loop(0, 64, place, 0)


def blend_kernel(hidden_ref, risen_ref, out_ref, first_ref, second_ref, grown, middle):
    risen = risen_ref[0]
    for k in range(1, 16):
        risen = risen + risen_ref[k]
    for b in range(4):
        v = risen[32 * b : 32 * b + 32]
        grown[pl.ds(0, 32, 2), :] = v
        grown[pl.ds(1, 32, 2), :] = v
        full = grown[...].reshape(2, 4, 1, 8, 128)
        turned = swap(full)
        lower = low_lanes(full.shape)
        for h in range(2):
            w = jnp.where(lower, full, turned) if h == 0 else jnp.where(lower, turned, full)
            for q in range(2):
                at = 64 * (2 * q + h)
                v = silu(hidden_ref[b, at : at + 64].reshape(4, 2, 8, 128) + w[q])
                out_ref[b, at : at + 64] = v.reshape(64, 128)
    fine_sends(out_ref, first_ref, second_ref, middle)


def fine_out_kernel(
    links_ref, own_ref, first_ref, second_ref, features_ref, weight_ref, bias_ref,
    out_ref, source, flat, high, low, middle,
):
    source[8] = jnp.zeros((256, 128), F32)
    source[2:6] = own_ref[...]
    fine_halo(first_ref, second_ref, source, middle)
    fine_rim(source, links_ref, high, low)
    bias = jnp.concatenate([bias_ref[...]] * 2, axis=1)
    for zz in range(4):
        r = product(fine_columns(high, zz), fine_columns(low, zz), weight_ref) + bias
        r = r.reshape(8, 32, 128)
        for p in range(2):
            v0 = r[:, 16 * p : 16 * p + 8].reshape(64, 128)
            v1 = r[:, 16 * p + 8 : 16 * p + 16].reshape(64, 128)
            lower = low_lanes(v0.shape)
            flat[p, pl.ds(2 * zz + 1, 64, 8), :] = jnp.where(lower, v0, swap(v1))
            flat[p, pl.ds(2 * zz, 64, 8), :] = jnp.where(lower, swap(v0), v1)
    for p in range(2):
        out_ref[2 * p : 2 * p + 2] = features_ref[2 * p : 2 * p + 2] + flat[p].T.reshape(2, 64, 512)


def exchanged(first, second):
    count = lax.axis_size(BOTH)
    inner = [(i, i ^ 1) for i in range(count)]
    outer = [(i, i + 1) for i in range(1, count - 1, 2)]
    outer += [(b, a) for a, b in outer]
    second = lax.ppermute(second, BOTH, outer)
    return lax.ppermute(first, BOTH, inner), second


def struct(*shape, dtype=F32):
    return jax.ShapeDtypeStruct(shape, dtype)


def call(kernel, out, scratch, specs, args, flops):
    return pl.pallas_call(
        kernel,
        out_shape=out,
        in_specs=specs,
        out_specs=jax.tree.map(lambda o: SMEM if o.dtype == jnp.int32 else VMEM, out),
        scratch_shapes=scratch,
        cost_estimate=pl.CostEstimate(flops=flops, bytes_accessed=1 << 21, transcendentals=0),
        compiler_params=pltpu.CompilerParams(vmem_limit_bytes=40 << 20),
    )(*args)


def per_device(
    features, fine_links, codes, coarse_links, fine_in_weight, fine_in_bias, down_weight,
    coarse_first_weight, coarse_first_bias, coarse_second_weight, coarse_second_bias,
    up_weight, fine_out_weight, fine_out_bias,
):
    fine_padded = [pltpu.VMEM((3, 5, 10, 32, 128), BF16)] * 2
    fine_source = pltpu.VMEM((9, 256, 128), F32)
    middle = pltpu.VMEM((192, 128), F32)
    brick, shell = struct(4, 256, 128), struct(2, 160, 128)

    own, first, second = call(
        turn_kernel,
        (brick, shell, shell),
        [pltpu.VMEM((512, 128), F32), middle],
        [VMEM],
        (features,),
        1 << 20,
    )
    first, second = exchanged(first, second)
    weight_in = call(
        first_weight_kernel, struct(2304, 256, dtype=BF16), [], [VMEM], (fine_in_weight,), 1 << 20
    )
    later = (coarse_first_weight, coarse_second_weight, down_weight, up_weight, fine_out_weight)
    weight_first, weight_second, down, up, weight_out = call(
        later_weights_kernel,
        (
            struct(3456, 256, dtype=BF16), struct(3456, 256, dtype=BF16),
            struct(128, 512, dtype=BF16), struct(256, 256, dtype=BF16),
            struct(2304, 256, dtype=BF16),
        ),
        [],
        [VMEM] * 5,
        later,
        1 << 30,
    )
    weight_in, weight_first, weight_second, down, up, weight_out = lax.optimization_barrier(
        (weight_in, weight_first, weight_second, down, up, weight_out)
    )
    hidden, pooled = call(
        fine_in_kernel,
        (brick, struct(16, 136, 128)),
        [fine_source, *fine_padded, pltpu.VMEM((256, 128), F32), middle],
        [SMEM, SMEM] + [VMEM] * 6,
        (codes, fine_links, coarse_links, own, first, second, weight_in, fine_in_bias[None]),
        2 * 1024 * 2304 * 384,
    )
    spread = lax.all_to_all(pooled, "dev", 0, 0, tiled=True)
    cubes, place, group_codes = call(
        edge_kernel,
        (struct(840, 128), struct(256, dtype=jnp.int32), struct(64, dtype=jnp.int32)),
        [
            pltpu.VMEM((16, 128), F32), pltpu.SMEM((16, 128), F32), pltpu.VMEM((2, 256, 128), F32),
            middle, pltpu.SemaphoreType.DMA,
        ],
        [VMEM],
        (spread,),
        1 << 20,
    )
    groups, devices = lax.axis_size("grp"), lax.axis_size("dev")
    edges = [(g * devices + k, (g + 1) * devices + k) for g in range(groups - 1) for k in (0, 1)]
    edges += [((g + 1) * devices + k, g * devices + k) for g in range(groups - 1) for k in (14, 15)]
    edge = lax.ppermute(cubes, BOTH, edges)
    based, near_links = call(
        base_kernel,
        (struct(11, 512, 128), struct(8, 128)),
        [pltpu.VMEM((2, 256, 128), F32)],
        [VMEM, SMEM, VMEM],
        (spread, place, down),
        1 << 28,
    )
    coarse_padded = [pltpu.VMEM((3, 10, 10, 16, 128), BF16)] * 2
    inner = call(
        inner_kernel,
        struct(2, 512, 128),
        coarse_padded,
        [SMEM] + [VMEM] * 3,
        (near_links, based, weight_first, coarse_first_bias[None]),
        2 * 1024 * 3456 * 384,
    )
    lifted = call(
        coarse_kernel,
        struct(64, 32, 128),
        [
            pltpu.VMEM((11, 512, 128), F32), *coarse_padded, pltpu.VMEM((7, 512, 128), F32), *coarse_padded,
            pltpu.VMEM((16, 32, 128), F32), pltpu.VMEM((8, 128), F32), pltpu.SMEM((8, 128), F32),
            pltpu.VMEM((256, 128), F32), middle, pltpu.SemaphoreType.DMA,
        ],
        [SMEM, VMEM, SMEM] + [VMEM] * 9,
        (
            coarse_links, near_links, group_codes, based, edge, inner, down, weight_first,
            coarse_first_bias[None], weight_second, coarse_second_bias[None], up,
        ),
        6 * 1024 * 3456 * 384,
    )
    risen = lax.all_to_all(lifted.reshape(16, 128, 128), "dev", 0, 0, tiled=True)
    blended, first, second = call(
        blend_kernel,
        (brick, shell, shell),
        [pltpu.VMEM((64, 128), F32), middle],
        [VMEM, VMEM],
        (hidden, risen),
        1 << 20,
    )
    first, second = exchanged(first, second)
    return call(
        fine_out_kernel,
        struct(4, 64, 512),
        [fine_source, pltpu.VMEM((2, 512, 128), F32), *fine_padded, middle],
        [SMEM] + [VMEM] * 6,
        (fine_links, blended, first, second, features, weight_out, fine_out_bias[None]),
        2 * 1024 * 2304 * 384,
    )


def solution(mesh):
    split_first = P(BOTH)
    placed = (split_first,) * 4 + (P(),) * 10
    return jax.shard_map(
        per_device,
        mesh=mesh,
        in_specs=placed,
        out_specs=split_first,
        check_vma=False,
    )
```

```python
import jax
import jax.numpy as jnp
from jax import lax
from jax.experimental import pallas as pl
from jax.experimental.pallas import tpu as pltpu
from jax.sharding import PartitionSpec as P

F32, BF16 = jnp.float32, jnp.bfloat16
BOTH = ("grp", "dev")
STEPS = (-1, 0, 1)
COLUMN = {
    offset: k
    for k, offset in enumerate(
        (x, y, z) for x in STEPS for y in STEPS for z in STEPS if (x, y, z) != (0, 0, 0)
    )
}
PLANE = {-1: (56, 8), 0: (0, 64), 1: (0, 8)}
CHUNKS = [(-1, 56, 1, 0), (0, 0, 2, 1), (0, 16, 2, 3), (0, 32, 2, 5), (0, 48, 2, 7), (1, 0, 1, 9)]
VMEM = pl.BlockSpec(memory_space=pltpu.VMEM)
SMEM = pl.BlockSpec(memory_space=pltpu.SMEM)


def silu(v):
    return v / (1.0 + jnp.exp(-v))


def split(v):
    high = v.astype(BF16)
    return high, (v - high.astype(F32)).astype(BF16)


def low_lanes(shape):
    return lax.broadcasted_iota(jnp.int32, shape, len(shape) - 1) < 64


def swap(v):
    return pltpu.roll(v, 64, v.ndim - 1)


def device_number():
    return lax.axis_index("grp") * lax.axis_size("dev") + lax.axis_index("dev")


def neighbours(links_ref, row, start, none):
    found = {}
    for offset, k in COLUMN.items():
        link = links_ref[row, k].astype(jnp.int32)
        found[offset] = jnp.where(link < 0, none, jnp.clip(link - start, 0, none))
    return found


def planes(source, brick, z, dx):
    at, count = PLANE[dx]
    return source[brick, 64 * z + at : 64 * z + at + count, :].reshape(count // 8, 8, 128)


def even_device():
    return device_number() % 2 == 0


def fine_pack(brick_ref, out_ref, middle):
    first, last = brick_ref[0:64], brick_ref[192:256]
    lower = low_lanes(first.shape)
    out_ref[0:64] = jnp.where(lower, last, first)
    middle[0:64] = jnp.where(lower, first, last)
    middle[64:192] = brick_ref[64:192]
    for k in range(3):
        out_ref[64 + 8 * k : 72 + 8 * k] = middle[64 * k : 64 * k + 8]
        out_ref[88 + 8 * k : 96 + 8 * k] = middle[64 * k + 56 : 64 * k + 64]
    out_ref[112:136] = middle[pl.ds(0, 24, 8), :]
    out_ref[136:160] = middle[pl.ds(7, 24, 8), :]


def fine_unpack(packed_ref, brick_ref, middle):
    middle[pl.ds(0, 24, 8), :] = packed_ref[112:136]
    middle[pl.ds(7, 24, 8), :] = packed_ref[136:160]
    for k in range(3):
        middle[64 * k : 64 * k + 8] = packed_ref[64 + 8 * k : 72 + 8 * k]
        middle[64 * k + 56 : 64 * k + 64] = packed_ref[88 + 8 * k : 96 + 8 * k]
    ends, inner = packed_ref[0:64], middle[0:64]
    lower = low_lanes(ends.shape)
    brick_ref[0:64] = jnp.where(lower, inner, ends)
    brick_ref[64:192] = middle[64:192]
    brick_ref[192:256] = jnp.where(lower, ends, inner)


def fine_halo(first_ref, second_ref, source, middle):
    even = even_device()
    for packed_ref, at in ((first_ref, jnp.where(even, 6, 0)), (second_ref, jnp.where(even, 0, 6))):
        for m in range(2):
            fine_unpack(packed_ref.at[m], source.at[at + m], middle)


def fine_sends(brick_ref, first_ref, second_ref, middle):
    even = even_device()
    for out_ref, at in ((first_ref, jnp.where(even, 2, 0)), (second_ref, jnp.where(even, 0, 2))):
        for m in range(2):
            fine_pack(brick_ref.at[at + m], out_ref.at[m], middle)


def shifted_rows(tile):
    below, here, above = tile(-1), tile(0), tile(1)
    axis = here.ndim - 2
    row = lax.broadcasted_iota(jnp.int32, here.shape, axis)
    return (
        pltpu.roll(jnp.where(row == 7, below, here), 1, axis),
        here,
        pltpu.roll(jnp.where(row == 0, above, here), 7, axis),
    )


def product(high, low, weight):
    both = jnp.dot(high, weight, preferred_element_type=F32)
    half = both.shape[1] // 2
    rest = jnp.dot(low, weight[:, :half], preferred_element_type=F32)
    return both[:, :half] + both[:, half:] + rest


def filter_data(a, b, c, d):
    return a - c, b + c, c - b, b - d


def filter_taps(a, b, c):
    return a, (a + b + c) * 0.5, (a - b + c) * 0.5, c


def filtered(high, low, columns, weight_ref):
    depth = weight_ref.shape[0] // 4
    m = [
        product(columns(high, k), columns(low, k), weight_ref[depth * k : depth * k + depth, :])
        for k in range(4)
    ]
    return m[0] + m[1] + m[2], m[1] - m[2] - m[3]


def fine_rim(source, links_ref, high, low):
    start = device_number() * 4 - 2
    for pair in range(2):
        found = []
        for b in (2 * pair, 2 * pair + 1):
            near = neighbours(links_ref, b, start, 8)
            near[0, 0, 0] = b + 2
            found.append(near)
        for k in range(5):
            rows = []
            for near in found:

                def tile(dy):
                    parts = []
                    for dx in STEPS:
                        first = near[dx, dy, -1 if k == 0 else 0]
                        second = near[dx, dy, 1 if k == 4 else 0]
                        a = planes(source, first, (k + 3) % 4, dx)
                        b = planes(source, second, k % 4, dx)
                        parts.append(jnp.where(low_lanes(a.shape), a, b))
                    return jnp.concatenate(parts, axis=0)

                rows.append(shifted_rows(tile))
            for j in range(3):
                both = jnp.concatenate([rows[0][j], rows[1][j]], axis=1).reshape(5, 2, 16, 128)
                parts = filter_data(both[:4, 0], both[:4, 1], both[1:, 0], both[1:, 1])
                for n, part in enumerate(parts):
                    h, l = split(part)
                    high[n, j, k, :, 16 * pair : 16 * pair + 16, :] = h
                    low[n, j, k, :, 16 * pair : 16 * pair + 16, :] = l


def fine_convolved(high, low, half, weight_ref, bias):
    def columns(padded, k):
        return jnp.concatenate(
            [
                padded[k, j, 2 * half + h : 2 * half + h + 2].reshape(256, 128)
                for j in range(3)
                for h in range(2)
            ],
            axis=1,
        )

    pair = [y.reshape(2, 4, 32, 128) for y in filtered(high, low, columns, weight_ref)]
    return jnp.stack(pair, axis=2).reshape(2, 8, 32, 128) + bias


def turn_kernel(features_ref, own_ref, first_ref, second_ref, flat, middle):
    for p in range(2):
        flat[...] = features_ref[2 * p : 2 * p + 2].reshape(128, 512).T
        for zz in range(4):
            odd = flat[pl.ds(2 * zz + 1, 64, 8), :]
            even = flat[pl.ds(2 * zz, 64, 8), :]
            lower = low_lanes(odd.shape)
            own_ref[2 * p, 64 * zz : 64 * zz + 64] = jnp.where(lower, odd, swap(even))
            own_ref[2 * p + 1, 64 * zz : 64 * zz + 64] = jnp.where(lower, swap(odd), even)
    fine_sends(own_ref, first_ref, second_ref, middle)


def fine_weight_rows(weight_ref, out_ref):
    taps = []
    for at in range(0, 1728, 128):
        part = weight_ref[:, at : min(at + 128, 1728)]
        turned = jnp.concatenate([part, part], axis=0).T
        taps += [turned[r : r + 64] for r in range(0, turned.shape[0], 64)]
    nothing = jnp.zeros((64, 128), F32)
    lower = low_lanes((64, 128))
    for j in range(3):
        for z in range(4):
            across = []
            for i in range(3):
                at = 3 * (3 * i + j) + z
                odd = taps[at - 1] if z >= 1 else nothing
                even = taps[at] if z <= 2 else nothing
                across.append(jnp.where(lower, odd, even))
            for n, part in enumerate(filter_taps(*across)):
                h, l = split(part)
                at = 768 * n + 256 * j + 64 * z
                out_ref[at : at + 64, 0:128] = h
                out_ref[at : at + 64, 128:256] = l


def coarse_weight_rows(weight_ref, out_ref):
    for n in range(9):
        taps = [weight_ref[:, 128 * t : 128 * t + 128].T for t in range(3 * n, 3 * n + 3)]
        for k, part in enumerate(filter_taps(*taps)):
            h, l = split(part)
            at = 1152 * k + 128 * n
            out_ref[at : at + 128, 0:128] = h
            out_ref[at : at + 128, 128:256] = l


def first_weight_kernel(weight_ref, out_ref):
    fine_weight_rows(weight_ref, out_ref)


def later_weights_kernel(
    first_ref, second_ref, down_ref, up_ref, fine_ref, first_out, second_out, down_out, up_out, fine_out
):
    coarse_weight_rows(first_ref, first_out)
    coarse_weight_rows(second_ref, second_out)
    fine_weight_rows(fine_ref, fine_out)
    nothing = jnp.zeros((64, 128), F32)
    h, l = split(jnp.concatenate([down_ref[...].T, nothing], axis=0))
    down_out[:, 0:128] = h
    down_out[:, 256:384] = l
    h, l = split(jnp.concatenate([nothing, down_ref[...].T], axis=0))
    down_out[:, 128:256] = h
    down_out[:, 384:512] = l
    both = jnp.concatenate([up_ref[...], up_ref[...]], axis=0).T
    lower = low_lanes(both.shape)
    for k in range(2):
        h, l = split(jnp.where(lower if k == 0 else ~lower, both, 0.0))
        up_out[128 * k : 128 * k + 128, 0:128] = h
        up_out[128 * k : 128 * k + 128, 128:256] = l


def fine_in_kernel(
    codes_ref, links_ref, coarse_links_ref, own_ref, first_ref, second_ref, weight_ref, bias_ref,
    hidden_ref, pooled_ref, source, high, low, sums, middle,
):
    source[8] = jnp.zeros((256, 128), F32)
    source[2:6] = own_ref[...]
    fine_halo(first_ref, second_ref, source, middle)
    fine_rim(source, links_ref, high, low)
    bias = jnp.concatenate([bias_ref[...]] * 2, axis=1)
    for half in range(2):
        r = silu(fine_convolved(high, low, half, weight_ref, bias))
        for h in range(2):
            at = 64 * (2 * half + h)
            for b in range(4):
                hidden_ref[b, at : at + 64] = r[h, :, 8 * b : 8 * b + 8].reshape(64, 128)
        r = r.reshape(2, 4, 2, 32, 128)
        r = r[:, :, 0] + r[:, :, 1]
        r = r + swap(r)
        both = jnp.where(low_lanes(r[0].shape), r[1], r[0])
        sums[128 * half : 128 * half + 128, :] = both.reshape(128, 128)
    means = (sums[pl.ds(0, 128, 2), :] + sums[pl.ds(1, 128, 2), :]) * 0.125
    for n in range(8):
        for b in range(4):
            at = (4 * n + b) * 4
            pooled_ref[0, 32 * b + 4 * n : 32 * b + 4 * n + 4, :] = means[at : at + 4]
    lane = lax.broadcasted_iota(jnp.int32, (8, 128), 1)
    named = jnp.zeros((8, 128), F32)
    for b in range(4):
        named = jnp.where(lane == b, codes_ref[b].astype(F32), named)
    pooled_ref[0, 128:136, :] = named
    pooled_ref[0, 129:131, 0:26] = coarse_links_ref[...].astype(F32)
    for k in range(1, 16):
        pooled_ref[k] = pooled_ref[0]


def cube_rows(all_ref, place_ref, code, store):
    for t in range(16):
        a, b, c = t // 4 % 2, t // 2 % 2, t % 2
        i = place_ref[code + t]
        at = jnp.maximum(i, 0)
        v = all_ref[at // 4, pl.ds(pl.multiple_of(at % 4 * 32, 32), 32), :]
        v = jnp.where(i >= 0, v, 0.0)
        for r in range(8):
            store(t // 8, (2 * c + r // 4) * 64 + (4 * a + r % 4) * 8 + 4 * b, v[4 * r : 4 * r + 4])


def edge_kernel(all_ref, cubes_ref, place_ref, codes_ref, held, spelled, cubes, middle, sem):
    held[...] = all_ref[:, 128, :]
    copy = pltpu.make_async_copy(held, spelled, sem)
    copy.start()
    me = lax.axis_index("dev")
    for t in range(256):
        place_ref[t] = -1
    copy.wait()
    for i in range(64):
        code = spelled[i // 4, i % 4].astype(jnp.int32)
        codes_ref[i] = code
        place_ref[code] = i
    cubes_ref[832:840] = all_ref[jnp.where(me < 8, 15, 0), 128:136, :]

    @pl.when((me < 2) | (me > 13))
    def _():
        def store(s, at, v):
            cubes_ref[256 * s + at : 256 * s + at + 4, :] = v

        cube_rows(all_ref, place_ref, jnp.where(me < 2, 15, 0) * 16, store)

        def hold(s, at, v):
            cubes[s, at : at + 4, :] = v

        cube_rows(all_ref, place_ref, jnp.where(me < 2, 14, 1) * 16, hold)
        for s in range(2):
            fine_pack(cubes.at[s], cubes_ref.at[512 + 160 * s : 672 + 160 * s], middle)


def bring_down(cubes, down_ref, source, n):
    h, l = split(cubes)
    based = product(h, l, down_ref[...])
    for z in range(8):
        k = 1 - z % 2
        source[n, 64 * z : 64 * z + 64] = based[64 * (z // 2) : 64 * (z // 2) + 64, 128 * k : 128 * k + 128]


def base_kernel(all_ref, place_ref, down_ref, out_ref, links_ref, cubes):
    me = lax.axis_index("dev")
    links_ref[...] = jnp.zeros((8, 128), F32)
    out_ref[10] = jnp.zeros((512, 128), F32)
    for n in range(5):
        owner = jnp.clip(me + (n - 2), 0, 15)

        def store(s, at, v):
            cubes[s, at : at + 4, :] = v

        cube_rows(all_ref, place_ref, owner * 16, store)
        for s in range(2):
            bring_down(cubes[s], down_ref, out_ref, 2 * n + s)
        if 1 <= n <= 3:
            links_ref[2 * n - 2 : 2 * n] = all_ref[owner, 129:131, :]


def coarse_rim(source, links_ref, row, home, start, none, high, low):
    found = []
    for s in range(2):
        near = neighbours(links_ref, row + s, start, none)
        near[0, 0, 0] = home + s
        found.append(near)
    for dx, at, count, room in CHUNKS:
        window = []
        for z in range(10):
            dz = -1 if z == 0 else 1 if z == 9 else 0
            begin = 64 * {-1: 7, 0: z - 1, 1: 0}[dz] + at
            rows = [
                shifted_rows(
                    lambda dy, near=near: source[near[dx, dy, dz], begin : begin + 8 * count, :].reshape(count, 8, 128)
                )
                for near in found
            ]
            window.append([jnp.concatenate([rows[0][j], rows[1][j]], axis=1) for j in range(3)])
            if z >= 3 and z % 2 == 1:
                for j in range(3):
                    for k, part in enumerate(filter_data(*[w[j] for w in window[z - 3 :]])):
                        h, l = split(part)
                        high[k, j, z // 2 - 1, room : room + count] = h
                        low[k, j, z // 2 - 1, room : room + count] = l


def coarse_convolved(high, low, half, weight_ref, bias):
    def columns(padded, k):
        return jnp.concatenate(
            [
                padded[k, j, 2 * half : 2 * half + 2, i : i + 8].reshape(256, 128)
                for i in range(3)
                for j in range(3)
            ],
            axis=1,
        )

    return [silu(y + bias) for y in filtered(high, low, columns, weight_ref)]


def coarse_first_pair(source, links_ref, pair, weight_ref, bias_ref, out_ref, n, high, low):
    coarse_rim(source, links_ref, 2 * pair, 2 * pair + 2, device_number() * 2 - 4, 10, high, low)
    for half in range(2):
        for odd, r in enumerate(coarse_convolved(high, low, half, weight_ref, bias_ref[...])):
            r = r.reshape(2, 8, 16, 128)
            for s in range(2):
                for h in range(2):
                    at = 64 * (4 * half + 2 * h + odd)
                    out_ref[n + s, at : at + 64] = r[h, :, 8 * s : 8 * s + 8].reshape(64, 128)


def inner_pair():
    return jnp.where(lax.axis_index("dev") < 8, 2, 0)


def inner_kernel(links_ref, based_ref, weight_ref, bias_ref, out_ref, high, low):
    coarse_first_pair(based_ref, links_ref, inner_pair(), weight_ref, bias_ref, out_ref, 0, high, low)


def coarse_kernel(
    links_ref, near_links_ref, codes_ref, based_ref, edge_ref, inner_ref, down_ref, first_weight_ref, first_bias_ref,
    weight_ref, bias_ref, up_ref, out_ref, source, high, low, seconds, high2, low2, octants, held, spelled,
    cubes, middle, sem,
):
    me = lax.axis_index("dev")
    held[...] = near_links_ref[...]

    @pl.when(me == 0)
    def _():
        held[0:2] = edge_ref[833:835]

    @pl.when(me == 15)
    def _():
        held[4:6] = edge_ref[833:835]

    copy = pltpu.make_async_copy(held, spelled, sem)
    copy.start()
    source[...] = based_ref[...]

    @pl.when((me < 2) | (me > 13))
    def _():
        at = jnp.where(me < 2, jnp.where(me == 0, 2, 0), jnp.where(me == 15, 6, 8))
        for s in range(2):
            bring_down(edge_ref[256 * s : 256 * s + 256], down_ref, source, at + s)

    @pl.when((me == 0) | (me == 15))
    def _():
        at = jnp.where(me == 0, 0, 8)
        for s in range(2):
            fine_unpack(edge_ref.at[512 + 160 * s : 672 + 160 * s], cubes, middle)
            bring_down(cubes[...], down_ref, source, at + s)

    seconds[6] = jnp.zeros((512, 128), F32)
    inner = inner_pair()
    for s in range(2):
        seconds[2 * inner + s] = inner_ref[s]
    copy.wait()
    outer = 2 - inner
    coarse_first_pair(source, spelled, outer, first_weight_ref, first_bias_ref, seconds, 2 * outer, high, low)
    coarse_first_pair(source, spelled, 1, first_weight_ref, first_bias_ref, seconds, 2, high2, low2)
    coarse_rim(seconds, links_ref, 0, 2, device_number() * 2 - 2, 6, high, low)
    for c in range(2):
        h, l = split(jnp.concatenate(coarse_convolved(high, low, c, weight_ref, bias_ref[...]), axis=1))
        lifted = product(h, l, up_ref[...])
        for t in range(c, 16, 2):
            s, a, b = t // 8, t // 4 % 2, t // 2 % 2
            for q in range(2):
                for x in range(4):
                    at = 128 * q + (4 * a + x) * 16 + 8 * s + 4 * b
                    octants[t, 16 * q + 4 * x : 16 * q + 4 * x + 4, :] = lifted[at : at + 4]
    base = lax.axis_index("dev") * 16

    def place(i, carry):
        local = codes_ref[i] - base
        known = (local >= 0) & (local < 16)
        v = octants[jnp.clip(local, 0, 15)]
        out_ref[i] = jnp.where(known, v, 0.0)
        return carry

    lax.fori_loop(0, 64, place, 0)


def blend_kernel(hidden_ref, risen_ref, out_ref, first_ref, second_ref, grown, middle):
    risen = risen_ref[0]
    for k in range(1, 16):
        risen = risen + risen_ref[k]
    for b in range(4):
        v = risen[32 * b : 32 * b + 32]
        grown[pl.ds(0, 32, 2), :] = v
        grown[pl.ds(1, 32, 2), :] = v
        full = grown[...].reshape(2, 4, 1, 8, 128)
        turned = swap(full)
        lower = low_lanes(full.shape)
        for h in range(2):
            w = jnp.where(lower, full, turned) if h == 0 else jnp.where(lower, turned, full)
            for q in range(2):
                at = 64 * (2 * q + h)
                v = silu(hidden_ref[b, at : at + 64].reshape(4, 2, 8, 128) + w[q])
                out_ref[b, at : at + 64] = v.reshape(64, 128)
    fine_sends(out_ref, first_ref, second_ref, middle)


def fine_out_kernel(
    links_ref, own_ref, first_ref, second_ref, features_ref, weight_ref, bias_ref,
    out_ref, source, flat, high, low, middle,
):
    source[8] = jnp.zeros((256, 128), F32)
    source[2:6] = own_ref[...]
    fine_halo(first_ref, second_ref, source, middle)
    fine_rim(source, links_ref, high, low)
    bias = jnp.concatenate([bias_ref[...]] * 2, axis=1)
    for zz in range(4):
        if zz % 2 == 0:
            both = fine_convolved(high, low, zz // 2, weight_ref, bias)
        r = both[zz % 2]
        for p in range(2):
            v0 = r[:, 16 * p : 16 * p + 8].reshape(64, 128)
            v1 = r[:, 16 * p + 8 : 16 * p + 16].reshape(64, 128)
            lower = low_lanes(v0.shape)
            flat[p, pl.ds(2 * zz + 1, 64, 8), :] = jnp.where(lower, v0, swap(v1))
            flat[p, pl.ds(2 * zz, 64, 8), :] = jnp.where(lower, swap(v0), v1)
    for p in range(2):
        out_ref[2 * p : 2 * p + 2] = features_ref[2 * p : 2 * p + 2] + flat[p].T.reshape(2, 64, 512)


def exchanged(first, second):
    count = lax.axis_size(BOTH)
    inner = [(i, i ^ 1) for i in range(count)]
    outer = [(i, i + 1) for i in range(1, count - 1, 2)]
    outer += [(b, a) for a, b in outer]
    second = lax.ppermute(second, BOTH, outer)
    return lax.ppermute(first, BOTH, inner), second


def struct(*shape, dtype=F32):
    return jax.ShapeDtypeStruct(shape, dtype)


def call(kernel, out, scratch, specs, args, flops):
    return pl.pallas_call(
        kernel,
        out_shape=out,
        in_specs=specs,
        out_specs=jax.tree.map(lambda o: SMEM if o.dtype == jnp.int32 else VMEM, out),
        scratch_shapes=scratch,
        cost_estimate=pl.CostEstimate(flops=flops, bytes_accessed=1 << 21, transcendentals=0),
        compiler_params=pltpu.CompilerParams(vmem_limit_bytes=40 << 20),
    )(*args)


def per_device(
    features, fine_links, codes, coarse_links, fine_in_weight, fine_in_bias, down_weight,
    coarse_first_weight, coarse_first_bias, coarse_second_weight, coarse_second_bias,
    up_weight, fine_out_weight, fine_out_bias,
):
    fine_padded = [pltpu.VMEM((4, 3, 5, 4, 32, 128), BF16)] * 2
    fine_source = pltpu.VMEM((9, 256, 128), F32)
    middle = pltpu.VMEM((192, 128), F32)
    brick, shell = struct(4, 256, 128), struct(2, 160, 128)

    own, first, second = call(
        turn_kernel,
        (brick, shell, shell),
        [pltpu.VMEM((512, 128), F32), middle],
        [VMEM],
        (features,),
        1 << 20,
    )
    first, second = exchanged(first, second)
    weight_in = call(
        first_weight_kernel, struct(3072, 256, dtype=BF16), [], [VMEM], (fine_in_weight,), 1 << 20
    )
    later = (coarse_first_weight, coarse_second_weight, down_weight, up_weight, fine_out_weight)
    weight_first, weight_second, down, up, weight_out = call(
        later_weights_kernel,
        (
            struct(4608, 256, dtype=BF16), struct(4608, 256, dtype=BF16),
            struct(128, 512, dtype=BF16), struct(256, 256, dtype=BF16),
            struct(3072, 256, dtype=BF16),
        ),
        [],
        [VMEM] * 5,
        later,
        1 << 30,
    )
    weight_in, weight_first, weight_second, down, up, weight_out = lax.optimization_barrier(
        (weight_in, weight_first, weight_second, down, up, weight_out)
    )
    hidden, pooled = call(
        fine_in_kernel,
        (brick, struct(16, 136, 128)),
        [fine_source, *fine_padded, pltpu.VMEM((256, 128), F32), middle],
        [SMEM, SMEM] + [VMEM] * 6,
        (codes, fine_links, coarse_links, own, first, second, weight_in, fine_in_bias[None]),
        2 * 1024 * 2304 * 384,
    )
    spread = lax.all_to_all(pooled, "dev", 0, 0, tiled=True)
    cubes, place, group_codes = call(
        edge_kernel,
        (struct(840, 128), struct(256, dtype=jnp.int32), struct(64, dtype=jnp.int32)),
        [
            pltpu.VMEM((16, 128), F32), pltpu.SMEM((16, 128), F32), pltpu.VMEM((2, 256, 128), F32),
            middle, pltpu.SemaphoreType.DMA,
        ],
        [VMEM],
        (spread,),
        1 << 20,
    )
    groups, devices = lax.axis_size("grp"), lax.axis_size("dev")
    edges = [(g * devices + k, (g + 1) * devices + k) for g in range(groups - 1) for k in (0, 1)]
    edges += [((g + 1) * devices + k, g * devices + k) for g in range(groups - 1) for k in (14, 15)]
    edge = lax.ppermute(cubes, BOTH, edges)
    based, near_links = call(
        base_kernel,
        (struct(11, 512, 128), struct(8, 128)),
        [pltpu.VMEM((2, 256, 128), F32)],
        [VMEM, SMEM, VMEM],
        (spread, place, down),
        1 << 28,
    )
    coarse_padded = [pltpu.VMEM((4, 3, 4, 10, 16, 128), BF16)] * 2
    inner = call(
        inner_kernel,
        struct(2, 512, 128),
        coarse_padded,
        [SMEM] + [VMEM] * 3,
        (near_links, based, weight_first, coarse_first_bias[None]),
        2 * 1024 * 3456 * 384,
    )
    lifted = call(
        coarse_kernel,
        struct(64, 32, 128),
        [
            pltpu.VMEM((11, 512, 128), F32), *coarse_padded, pltpu.VMEM((7, 512, 128), F32), *coarse_padded,
            pltpu.VMEM((16, 32, 128), F32), pltpu.VMEM((8, 128), F32), pltpu.SMEM((8, 128), F32),
            pltpu.VMEM((256, 128), F32), middle, pltpu.SemaphoreType.DMA,
        ],
        [SMEM, VMEM, SMEM] + [VMEM] * 9,
        (
            coarse_links, near_links, group_codes, based, edge, inner, down, weight_first,
            coarse_first_bias[None], weight_second, coarse_second_bias[None], up,
        ),
        6 * 1024 * 3456 * 384,
    )
    risen = lax.all_to_all(lifted.reshape(16, 128, 128), "dev", 0, 0, tiled=True)
    blended, first, second = call(
        blend_kernel,
        (brick, shell, shell),
        [pltpu.VMEM((64, 128), F32), middle],
        [VMEM, VMEM],
        (hidden, risen),
        1 << 20,
    )
    first, second = exchanged(first, second)
    return call(
        fine_out_kernel,
        struct(4, 64, 512),
        [fine_source, pltpu.VMEM((2, 512, 128), F32), *fine_padded, middle],
        [SMEM] + [VMEM] * 6,
        (fine_links, blended, first, second, features, weight_out, fine_out_bias[None]),
        2 * 1024 * 2304 * 384,
    )


def solution(mesh):
    split_first = P(BOTH)
    placed = (split_first,) * 4 + (P(),) * 10
    return jax.shard_map(
        per_device,
        mesh=mesh,
        in_specs=placed,
        out_specs=split_first,
        check_vma=False,
    )
```

```python
import jax
import jax.numpy as jnp
from jax import lax
from jax.experimental import pallas as pl
from jax.experimental.pallas import tpu as pltpu
from jax.sharding import PartitionSpec as P

F32, BF16 = jnp.float32, jnp.bfloat16
BOTH = ("grp", "dev")
STEPS = (-1, 0, 1)
COLUMN = {
    offset: k
    for k, offset in enumerate(
        (x, y, z) for x in STEPS for y in STEPS for z in STEPS if (x, y, z) != (0, 0, 0)
    )
}
PLANE = {-1: (56, 8), 0: (0, 64), 1: (0, 8)}
CHUNKS = [(-1, 56, 1, 0), (0, 0, 2, 1), (0, 16, 2, 3), (0, 32, 2, 5), (0, 48, 2, 7), (1, 0, 1, 9)]
VMEM = pl.BlockSpec(memory_space=pltpu.VMEM)
SMEM = pl.BlockSpec(memory_space=pltpu.SMEM)


def silu(v):
    return v / (1.0 + jnp.exp(-v))


def split(v):
    high = v.astype(BF16)
    return high, (v - high.astype(F32)).astype(BF16)


def low_lanes(shape):
    return lax.broadcasted_iota(jnp.int32, shape, len(shape) - 1) < 64


def swap(v):
    return pltpu.roll(v, 64, v.ndim - 1)


def device_number():
    return lax.axis_index("grp") * lax.axis_size("dev") + lax.axis_index("dev")


def neighbours(links_ref, row, start, none):
    found = {}
    for offset, k in COLUMN.items():
        link = links_ref[row, k].astype(jnp.int32)
        found[offset] = jnp.where(link < 0, none, jnp.clip(link - start, 0, none))
    return found


def planes(source, brick, z, dx):
    at, count = PLANE[dx]
    return source[brick, 64 * z + at : 64 * z + at + count, :].reshape(count // 8, 8, 128)


def even_device():
    return device_number() % 2 == 0


def fine_pack(brick_ref, out_ref, middle):
    first, last = brick_ref[0:64], brick_ref[192:256]
    lower = low_lanes(first.shape)
    out_ref[0:64] = jnp.where(lower, last, first)
    middle[0:64] = jnp.where(lower, first, last)
    middle[64:192] = brick_ref[64:192]
    for k in range(3):
        out_ref[64 + 8 * k : 72 + 8 * k] = middle[64 * k : 64 * k + 8]
        out_ref[88 + 8 * k : 96 + 8 * k] = middle[64 * k + 56 : 64 * k + 64]
    out_ref[112:136] = middle[pl.ds(0, 24, 8), :]
    out_ref[136:160] = middle[pl.ds(7, 24, 8), :]


def fine_unpack(packed_ref, brick_ref, middle):
    middle[pl.ds(0, 24, 8), :] = packed_ref[112:136]
    middle[pl.ds(7, 24, 8), :] = packed_ref[136:160]
    for k in range(3):
        middle[64 * k : 64 * k + 8] = packed_ref[64 + 8 * k : 72 + 8 * k]
        middle[64 * k + 56 : 64 * k + 64] = packed_ref[88 + 8 * k : 96 + 8 * k]
    ends, inner = packed_ref[0:64], middle[0:64]
    lower = low_lanes(ends.shape)
    brick_ref[0:64] = jnp.where(lower, inner, ends)
    brick_ref[64:192] = middle[64:192]
    brick_ref[192:256] = jnp.where(lower, ends, inner)


def fine_halo(first_ref, second_ref, source, middle):
    even = even_device()
    for packed_ref, at in ((first_ref, jnp.where(even, 6, 0)), (second_ref, jnp.where(even, 0, 6))):
        for m in range(2):
            fine_unpack(packed_ref.at[m], source.at[at + m], middle)


def fine_sends(brick_ref, first_ref, second_ref, middle):
    even = even_device()
    for out_ref, at in ((first_ref, jnp.where(even, 2, 0)), (second_ref, jnp.where(even, 0, 2))):
        for m in range(2):
            fine_pack(brick_ref.at[at + m], out_ref.at[m], middle)


def shifted_rows(tile):
    below, here, above = tile(-1), tile(0), tile(1)
    axis = here.ndim - 2
    row = lax.broadcasted_iota(jnp.int32, here.shape, axis)
    return (
        pltpu.roll(jnp.where(row == 7, below, here), 1, axis),
        here,
        pltpu.roll(jnp.where(row == 0, above, here), 7, axis),
    )


def product(high, low, weight):
    half = weight.shape[1] // 2
    again = jnp.concatenate([weight[:, :half], jnp.zeros((weight.shape[0], half), BF16)], axis=1)
    both = jnp.dot(
        jnp.concatenate([high, low], axis=1),
        jnp.concatenate([weight, again], axis=0),
        preferred_element_type=F32,
    )
    return both[:, :half] + both[:, half:]


def filter_data(a, b, c, d):
    return a - c, b + c, c - b, b - d


def filter_taps(a, b, c):
    return a, (a + b + c) * 0.5, (a - b + c) * 0.5, c


def filtered(high, low, columns, weight_ref):
    depth = weight_ref.shape[0] // 4
    m = [
        product(columns(high, k), columns(low, k), weight_ref[depth * k : depth * k + depth, :])
        for k in range(4)
    ]
    return m[0] + m[1] + m[2], m[1] - m[2] - m[3]


def fine_rim(source, links_ref, high, low):
    start = device_number() * 4 - 2
    for pair in range(2):
        found = []
        for b in (2 * pair, 2 * pair + 1):
            near = neighbours(links_ref, b, start, 8)
            near[0, 0, 0] = b + 2
            found.append(near)
        for k in range(5):
            rows = []
            for near in found:

                def tile(dy):
                    parts = []
                    for dx in STEPS:
                        first = near[dx, dy, -1 if k == 0 else 0]
                        second = near[dx, dy, 1 if k == 4 else 0]
                        a = planes(source, first, (k + 3) % 4, dx)
                        b = planes(source, second, k % 4, dx)
                        parts.append(jnp.where(low_lanes(a.shape), a, b))
                    return jnp.concatenate(parts, axis=0)

                rows.append(shifted_rows(tile))
            for j in range(3):
                both = jnp.concatenate([rows[0][j], rows[1][j]], axis=1).reshape(5, 2, 16, 128)
                parts = filter_data(both[:4, 0], both[:4, 1], both[1:, 0], both[1:, 1])
                for n, part in enumerate(parts):
                    h, l = split(part)
                    high[n, j, k, :, 16 * pair : 16 * pair + 16, :] = h
                    low[n, j, k, :, 16 * pair : 16 * pair + 16, :] = l


def fine_convolved(high, low, half, weight_ref, bias):
    def columns(padded, k):
        return jnp.concatenate(
            [
                padded[k, j, 2 * half + h : 2 * half + h + 2].reshape(256, 128)
                for j in range(3)
                for h in range(2)
            ],
            axis=1,
        )

    pair = [y.reshape(2, 4, 32, 128) for y in filtered(high, low, columns, weight_ref)]
    return jnp.stack(pair, axis=2).reshape(2, 8, 32, 128) + bias


def turn_kernel(features_ref, own_ref, first_ref, second_ref, flat, middle):
    for p in range(2):
        flat[...] = features_ref[2 * p : 2 * p + 2].reshape(128, 512).T
        for zz in range(4):
            odd = flat[pl.ds(2 * zz + 1, 64, 8), :]
            even = flat[pl.ds(2 * zz, 64, 8), :]
            lower = low_lanes(odd.shape)
            own_ref[2 * p, 64 * zz : 64 * zz + 64] = jnp.where(lower, odd, swap(even))
            own_ref[2 * p + 1, 64 * zz : 64 * zz + 64] = jnp.where(lower, swap(odd), even)
    fine_sends(own_ref, first_ref, second_ref, middle)


def fine_weight_rows(weight_ref, out_ref):
    taps = []
    for at in range(0, 1728, 128):
        part = weight_ref[:, at : min(at + 128, 1728)]
        turned = jnp.concatenate([part, part], axis=0).T
        taps += [turned[r : r + 64] for r in range(0, turned.shape[0], 64)]
    nothing = jnp.zeros((64, 128), F32)
    lower = low_lanes((64, 128))
    for j in range(3):
        for z in range(4):
            across = []
            for i in range(3):
                at = 3 * (3 * i + j) + z
                odd = taps[at - 1] if z >= 1 else nothing
                even = taps[at] if z <= 2 else nothing
                across.append(jnp.where(lower, odd, even))
            for n, part in enumerate(filter_taps(*across)):
                h, l = split(part)
                at = 768 * n + 256 * j + 64 * z
                out_ref[at : at + 64, 0:128] = h
                out_ref[at : at + 64, 128:256] = l


def coarse_weight_rows(weight_ref, out_ref):
    for n in range(9):
        taps = [weight_ref[:, 128 * t : 128 * t + 128].T for t in range(3 * n, 3 * n + 3)]
        for k, part in enumerate(filter_taps(*taps)):
            h, l = split(part)
            at = 1152 * k + 128 * n
            out_ref[at : at + 128, 0:128] = h
            out_ref[at : at + 128, 128:256] = l


def fine_weight_kernel(weight_ref, out_ref):
    fine_weight_rows(weight_ref, out_ref)


def down_weights_kernel(first_ref, down_ref, first_out, down_out):
    coarse_weight_rows(first_ref, first_out)
    nothing = jnp.zeros((64, 128), F32)
    for k, rows in enumerate(([down_ref[...], nothing], [nothing, down_ref[...]])):
        h, l = split(jnp.concatenate(rows, axis=0))
        down_out[:, 128 * k : 128 * k + 128] = h
        down_out[:, 256 + 128 * k : 384 + 128 * k] = l


def up_weights_kernel(second_ref, up_ref, second_out, up_out):
    coarse_weight_rows(second_ref, second_out)
    both = jnp.concatenate([up_ref[...], up_ref[...]], axis=0).T
    lower = low_lanes(both.shape)
    for k in range(2):
        h, l = split(jnp.where(lower if k == 0 else ~lower, both, 0.0))
        up_out[128 * k : 128 * k + 128, 0:128] = h
        up_out[128 * k : 128 * k + 128, 128:256] = l


def fine_in_kernel(
    codes_ref, links_ref, coarse_links_ref, own_ref, second_ref, first_ref, weight_ref, bias_ref,
    hidden_ref, pooled_ref, source, high, low, sums, middle,
):
    source[8] = jnp.zeros((256, 128), F32)
    source[2:6] = own_ref[...]
    fine_halo(first_ref, second_ref, source, middle)
    fine_rim(source, links_ref, high, low)
    bias = jnp.concatenate([bias_ref[...]] * 2, axis=1)
    for half in range(2):
        r = silu(fine_convolved(high, low, half, weight_ref, bias))
        for h in range(2):
            at = 64 * (2 * half + h)
            for b in range(4):
                hidden_ref[b, at : at + 64] = r[h, :, 8 * b : 8 * b + 8].reshape(64, 128)
        r = r.reshape(2, 4, 2, 32, 128)
        r = r[:, :, 0] + r[:, :, 1]
        r = r + swap(r)
        both = jnp.where(low_lanes(r[0].shape), r[1], r[0])
        sums[128 * half : 128 * half + 128, :] = both.reshape(128, 128)
    means = (sums[pl.ds(0, 128, 2), :] + sums[pl.ds(1, 128, 2), :]) * 0.125
    for n in range(8):
        for b in range(4):
            at = (4 * n + b) * 4
            pooled_ref[0, 32 * b + 4 * n : 32 * b + 4 * n + 4, :] = means[at : at + 4]
    lane = lax.broadcasted_iota(jnp.int32, (8, 128), 1)
    named = jnp.zeros((8, 128), F32)
    for b in range(4):
        named = jnp.where(lane == b, codes_ref[b].astype(F32), named)
    pooled_ref[0, 128:136, :] = named
    pooled_ref[0, 129:131, 0:26] = coarse_links_ref[...].astype(F32)
    for k in range(1, 16):
        pooled_ref[k] = pooled_ref[0]


def cube_rows(all_ref, place_ref, code, store):
    for t in range(16):
        a, b, c = t // 4 % 2, t // 2 % 2, t % 2
        i = place_ref[code + t]
        at = jnp.maximum(i, 0)
        v = all_ref[at // 4, pl.ds(pl.multiple_of(at % 4 * 32, 32), 32), :]
        v = jnp.where(i >= 0, v, 0.0)
        for r in range(8):
            store(t // 8, (2 * c + r // 4) * 64 + (4 * a + r % 4) * 8 + 4 * b, v[4 * r : 4 * r + 4])


def edge_kernel(all_ref, cubes_ref, place_ref, codes_ref, held, spelled, cubes, middle, sem):
    held[...] = all_ref[:, 128, :]
    copy = pltpu.make_async_copy(held, spelled, sem)
    copy.start()
    me = lax.axis_index("dev")
    for t in range(256):
        place_ref[t] = -1
    copy.wait()
    for i in range(64):
        code = spelled[i // 4, i % 4].astype(jnp.int32)
        codes_ref[i] = code
        place_ref[code] = i
    cubes_ref[832:840] = all_ref[jnp.where(me < 8, 15, 0), 128:136, :]

    @pl.when((me < 2) | (me > 13))
    def _():
        def store(s, at, v):
            cubes_ref[256 * s + at : 256 * s + at + 4, :] = v

        cube_rows(all_ref, place_ref, jnp.where(me < 2, 15, 0) * 16, store)

        def hold(s, at, v):
            cubes[s, at : at + 4, :] = v

        cube_rows(all_ref, place_ref, jnp.where(me < 2, 14, 1) * 16, hold)
        for s in range(2):
            fine_pack(cubes.at[s], cubes_ref.at[512 + 160 * s : 672 + 160 * s], middle)


def bring_down(cubes, down_ref, source, n):
    h, l = split(cubes)
    based = product(h, l, down_ref[...])
    for z in range(8):
        k = 1 - z % 2
        source[n, 64 * z : 64 * z + 64] = based[64 * (z // 2) : 64 * (z // 2) + 64, 128 * k : 128 * k + 128]


def base_kernel(all_ref, place_ref, down_ref, out_ref, links_ref, cubes):
    me = lax.axis_index("dev")
    links_ref[...] = jnp.zeros((8, 128), F32)
    out_ref[10] = jnp.zeros((512, 128), F32)
    for n in range(5):
        owner = jnp.clip(me + (n - 2), 0, 15)

        def store(s, at, v):
            cubes[s, at : at + 4, :] = v

        cube_rows(all_ref, place_ref, owner * 16, store)
        for s in range(2):
            bring_down(cubes[s], down_ref, out_ref, 2 * n + s)
        if 1 <= n <= 3:
            links_ref[2 * n - 2 : 2 * n] = all_ref[owner, 129:131, :]


def coarse_rim(source, links_ref, row, home, start, none, high, low):
    found = []
    for s in range(2):
        near = neighbours(links_ref, row + s, start, none)
        near[0, 0, 0] = home + s
        found.append(near)
    for dx, at, count, room in CHUNKS:
        window = []
        for z in range(10):
            dz = -1 if z == 0 else 1 if z == 9 else 0
            begin = 64 * {-1: 7, 0: z - 1, 1: 0}[dz] + at
            rows = [
                shifted_rows(
                    lambda dy, near=near: source[near[dx, dy, dz], begin : begin + 8 * count, :].reshape(count, 8, 128)
                )
                for near in found
            ]
            window.append([jnp.concatenate([rows[0][j], rows[1][j]], axis=1) for j in range(3)])
            if z >= 3 and z % 2 == 1:
                for j in range(3):
                    for k, part in enumerate(filter_data(*[w[j] for w in window[z - 3 :]])):
                        h, l = split(part)
                        high[k, j, z // 2 - 1, room : room + count] = h
                        low[k, j, z // 2 - 1, room : room + count] = l


def coarse_convolved(high, low, half, weight_ref, bias):
    def columns(padded, k):
        return jnp.concatenate(
            [
                padded[k, j, 2 * half : 2 * half + 2, i : i + 8].reshape(256, 128)
                for i in range(3)
                for j in range(3)
            ],
            axis=1,
        )

    return [silu(y + bias) for y in filtered(high, low, columns, weight_ref)]


def coarse_first_pair(source, links_ref, pair, weight_ref, bias_ref, out_ref, n, high, low):
    coarse_rim(source, links_ref, 2 * pair, 2 * pair + 2, device_number() * 2 - 4, 10, high, low)
    for half in range(2):
        for odd, r in enumerate(coarse_convolved(high, low, half, weight_ref, bias_ref[...])):
            r = r.reshape(2, 8, 16, 128)
            for s in range(2):
                for h in range(2):
                    at = 64 * (4 * half + 2 * h + odd)
                    out_ref[n + s, at : at + 64] = r[h, :, 8 * s : 8 * s + 8].reshape(64, 128)


def inner_pair():
    return jnp.where(lax.axis_index("dev") < 8, 2, 0)


def inner_kernel(links_ref, based_ref, weight_ref, bias_ref, out_ref, high, low):
    coarse_first_pair(based_ref, links_ref, inner_pair(), weight_ref, bias_ref, out_ref, 0, high, low)


def coarse_kernel(
    links_ref, near_links_ref, codes_ref, based_ref, edge_ref, inner_ref, down_ref, first_weight_ref, first_bias_ref,
    weight_ref, bias_ref, up_ref, out_ref, source, high, low, seconds, high2, low2, octants, held, spelled,
    cubes, middle, sem,
):
    me = lax.axis_index("dev")
    held[...] = near_links_ref[...]

    @pl.when(me == 0)
    def _():
        held[0:2] = edge_ref[833:835]

    @pl.when(me == 15)
    def _():
        held[4:6] = edge_ref[833:835]

    copy = pltpu.make_async_copy(held, spelled, sem)
    copy.start()
    source[...] = based_ref[...]

    @pl.when((me < 2) | (me > 13))
    def _():
        at = jnp.where(me < 2, jnp.where(me == 0, 2, 0), jnp.where(me == 15, 6, 8))
        for s in range(2):
            bring_down(edge_ref[256 * s : 256 * s + 256], down_ref, source, at + s)

    @pl.when((me == 0) | (me == 15))
    def _():
        at = jnp.where(me == 0, 0, 8)
        for s in range(2):
            fine_unpack(edge_ref.at[512 + 160 * s : 672 + 160 * s], cubes, middle)
            bring_down(cubes[...], down_ref, source, at + s)

    seconds[6] = jnp.zeros((512, 128), F32)
    inner = inner_pair()
    for s in range(2):
        seconds[2 * inner + s] = inner_ref[s]
    copy.wait()
    outer = 2 - inner
    coarse_first_pair(source, spelled, outer, first_weight_ref, first_bias_ref, seconds, 2 * outer, high, low)
    coarse_first_pair(source, spelled, 1, first_weight_ref, first_bias_ref, seconds, 2, high2, low2)
    coarse_rim(seconds, links_ref, 0, 2, device_number() * 2 - 2, 6, high, low)
    for c in range(2):
        h, l = split(jnp.concatenate(coarse_convolved(high, low, c, weight_ref, bias_ref[...]), axis=1))
        lifted = product(h, l, up_ref[...])
        for t in range(c, 16, 2):
            s, a, b = t // 8, t // 4 % 2, t // 2 % 2
            for q in range(2):
                for x in range(4):
                    at = 128 * q + (4 * a + x) * 16 + 8 * s + 4 * b
                    octants[t, 16 * q + 4 * x : 16 * q + 4 * x + 4, :] = lifted[at : at + 4]
    base = lax.axis_index("dev") * 16

    def place(i, carry):
        local = codes_ref[i] - base
        known = (local >= 0) & (local < 16)
        v = octants[jnp.clip(local, 0, 15)]
        out_ref[i] = jnp.where(known, v, 0.0)
        return carry

    lax.fori_loop(0, 64, place, 0)


def blend_kernel(hidden_ref, risen_ref, out_ref, first_ref, second_ref, grown, middle):
    risen = risen_ref[0]
    for k in range(1, 16):
        risen = risen + risen_ref[k]
    for b in range(4):
        v = risen[32 * b : 32 * b + 32]
        grown[pl.ds(0, 32, 2), :] = v
        grown[pl.ds(1, 32, 2), :] = v
        full = grown[...].reshape(2, 4, 1, 8, 128)
        turned = swap(full)
        lower = low_lanes(full.shape)
        for h in range(2):
            w = jnp.where(lower, full, turned) if h == 0 else jnp.where(lower, turned, full)
            for q in range(2):
                at = 64 * (2 * q + h)
                v = silu(hidden_ref[b, at : at + 64].reshape(4, 2, 8, 128) + w[q])
                out_ref[b, at : at + 64] = v.reshape(64, 128)
    fine_sends(out_ref, first_ref, second_ref, middle)


def fine_out_kernel(
    links_ref, own_ref, second_ref, first_ref, features_ref, weight_ref, bias_ref,
    out_ref, source, flat, high, low, middle,
):
    source[8] = jnp.zeros((256, 128), F32)
    source[2:6] = own_ref[...]
    fine_halo(first_ref, second_ref, source, middle)
    fine_rim(source, links_ref, high, low)
    bias = jnp.concatenate([bias_ref[...]] * 2, axis=1)
    for zz in range(4):
        if zz % 2 == 0:
            both = fine_convolved(high, low, zz // 2, weight_ref, bias)
        r = both[zz % 2]
        for p in range(2):
            v0 = r[:, 16 * p : 16 * p + 8].reshape(64, 128)
            v1 = r[:, 16 * p + 8 : 16 * p + 16].reshape(64, 128)
            lower = low_lanes(v0.shape)
            flat[p, pl.ds(2 * zz + 1, 64, 8), :] = jnp.where(lower, v0, swap(v1))
            flat[p, pl.ds(2 * zz, 64, 8), :] = jnp.where(lower, swap(v0), v1)
    for p in range(2):
        out_ref[2 * p : 2 * p + 2] = features_ref[2 * p : 2 * p + 2] + flat[p].T.reshape(2, 64, 512)


def exchanged(first, second):
    count = lax.axis_size(BOTH)
    inner = [(i, i ^ 1) for i in range(count)]
    outer = [(i, i + 1) for i in range(1, count - 1, 2)]
    outer += [(b, a) for a, b in outer]
    second = lax.ppermute(second, BOTH, outer)
    return lax.ppermute(first, BOTH, inner), second


def struct(*shape, dtype=F32):
    return jax.ShapeDtypeStruct(shape, dtype)


def call(kernel, out, scratch, specs, args, flops):
    return pl.pallas_call(
        kernel,
        out_shape=out,
        in_specs=specs,
        out_specs=jax.tree.map(lambda o: SMEM if o.dtype == jnp.int32 else VMEM, out),
        scratch_shapes=scratch,
        cost_estimate=pl.CostEstimate(flops=flops, bytes_accessed=1 << 21, transcendentals=0),
        compiler_params=pltpu.CompilerParams(vmem_limit_bytes=40 << 20),
    )(*args)


def per_device(
    features, fine_links, codes, coarse_links, fine_in_weight, fine_in_bias, down_weight,
    coarse_first_weight, coarse_first_bias, coarse_second_weight, coarse_second_bias,
    up_weight, fine_out_weight, fine_out_bias,
):
    fine_padded = [pltpu.VMEM((4, 3, 5, 4, 32, 128), BF16)] * 2
    fine_source = pltpu.VMEM((9, 256, 128), F32)
    middle = pltpu.VMEM((192, 128), F32)
    brick, shell = struct(4, 256, 128), struct(2, 160, 128)

    own, first, second = call(
        turn_kernel,
        (brick, shell, shell),
        [pltpu.VMEM((512, 128), F32), middle],
        [VMEM],
        (features,),
        1 << 20,
    )
    first, second = exchanged(first, second)
    fine_rows, coarse_rows = struct(3072, 256, dtype=BF16), struct(4608, 256, dtype=BF16)
    weight_in = call(fine_weight_kernel, fine_rows, [], [VMEM], (fine_in_weight,), 1 << 20)
    weight_first, down = call(
        down_weights_kernel,
        (coarse_rows, struct(128, 512, dtype=BF16)),
        [],
        [VMEM] * 2,
        (coarse_first_weight, down_weight.T),
        1 << 20,
    )
    weight_second, up = call(
        up_weights_kernel,
        (coarse_rows, struct(256, 256, dtype=BF16)),
        [],
        [VMEM] * 2,
        (coarse_second_weight, up_weight),
        1 << 20,
    )
    weight_in, weight_first, down, weight_second, up = lax.optimization_barrier(
        (weight_in, weight_first, down, weight_second, up)
    )
    hidden, pooled = call(
        fine_in_kernel,
        (brick, struct(16, 136, 128)),
        [fine_source, *fine_padded, pltpu.VMEM((256, 128), F32), middle],
        [SMEM, SMEM] + [VMEM] * 6,
        (codes, fine_links, coarse_links, own, second, first, weight_in, fine_in_bias[None]),
        2 * 1024 * 2304 * 384,
    )
    spread = lax.all_to_all(pooled, "dev", 0, 0, tiled=True)
    cubes, place, group_codes = call(
        edge_kernel,
        (struct(840, 128), struct(256, dtype=jnp.int32), struct(64, dtype=jnp.int32)),
        [
            pltpu.VMEM((16, 128), F32), pltpu.SMEM((16, 128), F32), pltpu.VMEM((2, 256, 128), F32),
            middle, pltpu.SemaphoreType.DMA,
        ],
        [VMEM],
        (spread,),
        1 << 20,
    )
    groups, devices = lax.axis_size("grp"), lax.axis_size("dev")
    edges = [(g * devices + k, (g + 1) * devices + k) for g in range(groups - 1) for k in (0, 1)]
    edges += [((g + 1) * devices + k, g * devices + k) for g in range(groups - 1) for k in (14, 15)]
    edge = lax.ppermute(cubes, BOTH, edges)
    based, near_links = call(
        base_kernel,
        (struct(11, 512, 128), struct(8, 128)),
        [pltpu.VMEM((2, 256, 128), F32)],
        [VMEM, SMEM, VMEM],
        (spread, place, down),
        1 << 28,
    )
    coarse_padded = [pltpu.VMEM((4, 3, 4, 10, 16, 128), BF16)] * 2
    inner = call(
        inner_kernel,
        struct(2, 512, 128),
        coarse_padded,
        [SMEM] + [VMEM] * 3,
        (near_links, based, weight_first, coarse_first_bias[None]),
        2 * 1024 * 3456 * 384,
    )
    lifted = call(
        coarse_kernel,
        struct(64, 32, 128),
        [
            pltpu.VMEM((11, 512, 128), F32), *coarse_padded, pltpu.VMEM((7, 512, 128), F32), *coarse_padded,
            pltpu.VMEM((16, 32, 128), F32), pltpu.VMEM((8, 128), F32), pltpu.SMEM((8, 128), F32),
            pltpu.VMEM((256, 128), F32), middle, pltpu.SemaphoreType.DMA,
        ],
        [SMEM, VMEM, SMEM] + [VMEM] * 9,
        (
            coarse_links, near_links, group_codes, based, edge, inner, down, weight_first,
            coarse_first_bias[None], weight_second, coarse_second_bias[None], up,
        ),
        6 * 1024 * 3456 * 384,
    )
    risen = lax.all_to_all(lifted.reshape(16, 128, 128), "dev", 0, 0, tiled=True)
    blended, first, second = call(
        blend_kernel,
        (brick, shell, shell),
        [pltpu.VMEM((64, 128), F32), middle],
        [VMEM, VMEM],
        (hidden, risen),
        1 << 20,
    )
    first, second, out_raw = lax.optimization_barrier((first, second, fine_out_weight))
    weight_out = call(fine_weight_kernel, fine_rows, [], [VMEM], (out_raw,), 1 << 20)
    first, second = exchanged(first, second)
    return call(
        fine_out_kernel,
        struct(4, 64, 512),
        [fine_source, pltpu.VMEM((2, 512, 128), F32), *fine_padded, middle],
        [SMEM] + [VMEM] * 6,
        (fine_links, blended, second, first, features, weight_out, fine_out_bias[None]),
        2 * 1024 * 2304 * 384,
    )


def solution(mesh):
    split_first = P(BOTH)
    placed = (split_first,) * 4 + (P(),) * 10
    return jax.shard_map(
        per_device,
        mesh=mesh,
        in_specs=placed,
        out_specs=split_first,
        check_vma=False,
    )
```

```python
import jax
import jax.numpy as jnp
from jax import lax
from jax.experimental import pallas as pl
from jax.experimental.pallas import tpu as pltpu
from jax.sharding import PartitionSpec as P

F32, BF16 = jnp.float32, jnp.bfloat16
BOTH = ("grp", "dev")
STEPS = (-1, 0, 1)
COLUMN = {
    offset: k
    for k, offset in enumerate(
        (x, y, z) for x in STEPS for y in STEPS for z in STEPS if (x, y, z) != (0, 0, 0)
    )
}
PLANE = {-1: (56, 8), 0: (0, 64), 1: (0, 8)}
CHUNKS = [(-1, 56, 1, 0), (0, 0, 2, 1), (0, 16, 2, 3), (0, 32, 2, 5), (0, 48, 2, 7), (1, 0, 1, 9)]
VMEM = pl.BlockSpec(memory_space=pltpu.VMEM)
SMEM = pl.BlockSpec(memory_space=pltpu.SMEM)


def silu(v):
    return v / (1.0 + jnp.exp(-v))


def split(v):
    high = v.astype(BF16)
    return high, (v - high.astype(F32)).astype(BF16)


def low_lanes(shape):
    return lax.broadcasted_iota(jnp.int32, shape, len(shape) - 1) < 64


def swap(v):
    return pltpu.roll(v, 64, v.ndim - 1)


def device_number():
    return lax.axis_index("grp") * lax.axis_size("dev") + lax.axis_index("dev")


def neighbours(links_ref, row, start, none):
    found = {}
    for offset, k in COLUMN.items():
        link = links_ref[row, k].astype(jnp.int32)
        found[offset] = jnp.where(link < 0, none, jnp.clip(link - start, 0, none))
    return found


def planes(source, brick, z, dx):
    at, count = PLANE[dx]
    return source[brick, 64 * z + at : 64 * z + at + count, :].reshape(count // 8, 8, 128)


def even_device():
    return device_number() % 2 == 0


def fine_pack(brick_ref, out_ref, middle):
    first, last = brick_ref[0:64], brick_ref[192:256]
    lower = low_lanes(first.shape)
    out_ref[0:64] = jnp.where(lower, last, first)
    middle[0:64] = jnp.where(lower, first, last)
    middle[64:192] = brick_ref[64:192]
    for k in range(3):
        out_ref[64 + 8 * k : 72 + 8 * k] = middle[64 * k : 64 * k + 8]
        out_ref[88 + 8 * k : 96 + 8 * k] = middle[64 * k + 56 : 64 * k + 64]
    out_ref[112:136] = middle[pl.ds(0, 24, 8), :]
    out_ref[136:160] = middle[pl.ds(7, 24, 8), :]


def fine_unpack(packed_ref, brick_ref, middle):
    middle[pl.ds(0, 24, 8), :] = packed_ref[112:136]
    middle[pl.ds(7, 24, 8), :] = packed_ref[136:160]
    for k in range(3):
        middle[64 * k : 64 * k + 8] = packed_ref[64 + 8 * k : 72 + 8 * k]
        middle[64 * k + 56 : 64 * k + 64] = packed_ref[88 + 8 * k : 96 + 8 * k]
    ends, inner = packed_ref[0:64], middle[0:64]
    lower = low_lanes(ends.shape)
    brick_ref[0:64] = jnp.where(lower, inner, ends)
    brick_ref[64:192] = middle[64:192]
    brick_ref[192:256] = jnp.where(lower, ends, inner)


def fine_halo(first_ref, second_ref, source, middle):
    even = even_device()
    for packed_ref, at in ((first_ref, jnp.where(even, 6, 0)), (second_ref, jnp.where(even, 0, 6))):
        for m in range(2):
            fine_unpack(packed_ref.at[m], source.at[at + m], middle)


def fine_sends(brick_ref, first_ref, second_ref, middle):
    even = even_device()
    for out_ref, at in ((first_ref, jnp.where(even, 2, 0)), (second_ref, jnp.where(even, 0, 2))):
        for m in range(2):
            fine_pack(brick_ref.at[at + m], out_ref.at[m], middle)


def shifted_rows(tile):
    below, here, above = tile(-1), tile(0), tile(1)
    axis = here.ndim - 2
    row = lax.broadcasted_iota(jnp.int32, here.shape, axis)
    return (
        pltpu.roll(jnp.where(row == 7, below, here), 1, axis),
        here,
        pltpu.roll(jnp.where(row == 0, above, here), 7, axis),
    )


def product(high, low, weight):
    half = weight.shape[1] // 2
    again = jnp.concatenate([weight[:, :half], jnp.zeros((weight.shape[0], half), BF16)], axis=1)
    both = jnp.dot(
        jnp.concatenate([high, low], axis=1),
        jnp.concatenate([weight, again], axis=0),
        preferred_element_type=F32,
    )
    return both[:, :half] + both[:, half:]


def filter_data(a, b, c, d):
    return a - c, b + c, c - b, b - d


def filter_taps(a, b, c):
    return a, (a + b + c) * 0.5, (a - b + c) * 0.5, c


def filtered(high, low, columns, weight_ref):
    depth = weight_ref.shape[0] // 4
    m = [
        product(columns(high, k), columns(low, k), weight_ref[depth * k : depth * k + depth, :])
        for k in range(4)
    ]
    return m[0] + m[1] + m[2], m[1] - m[2] - m[3]


def fine_rim(source, links_ref, high, low):
    start = device_number() * 4 - 2
    for pair in range(2):
        found = []
        for b in (2 * pair, 2 * pair + 1):
            near = neighbours(links_ref, b, start, 8)
            near[0, 0, 0] = b + 2
            found.append(near)
        for k in range(5):
            rows = []
            for near in found:

                def tile(dy):
                    parts = []
                    for dx in STEPS:
                        first = near[dx, dy, -1 if k == 0 else 0]
                        second = near[dx, dy, 1 if k == 4 else 0]
                        a = planes(source, first, (k + 3) % 4, dx)
                        b = planes(source, second, k % 4, dx)
                        parts.append(jnp.where(low_lanes(a.shape), a, b))
                    return jnp.concatenate(parts, axis=0)

                rows.append(shifted_rows(tile))
            for j in range(3):
                both = jnp.concatenate([rows[0][j], rows[1][j]], axis=1).reshape(5, 2, 16, 128)
                parts = filter_data(both[:4, 0], both[:4, 1], both[1:, 0], both[1:, 1])
                for n, part in enumerate(parts):
                    h, l = split(part)
                    high[n, j, k, :, 16 * pair : 16 * pair + 16, :] = h
                    low[n, j, k, :, 16 * pair : 16 * pair + 16, :] = l


def fine_convolved(high, low, half, weight_ref, bias):
    def columns(padded, k):
        return jnp.concatenate(
            [
                padded[k, j, 2 * half + h : 2 * half + h + 2].reshape(256, 128)
                for j in range(3)
                for h in range(2)
            ],
            axis=1,
        )

    pair = [y.reshape(2, 4, 32, 128) for y in filtered(high, low, columns, weight_ref)]
    return jnp.stack(pair, axis=2).reshape(2, 8, 32, 128) + bias


def turn_kernel(features_ref, own_ref, first_ref, second_ref, flat, middle):
    for p in range(2):
        flat[...] = features_ref[2 * p : 2 * p + 2].reshape(128, 512).T
        for zz in range(4):
            odd = flat[pl.ds(2 * zz + 1, 64, 8), :]
            even = flat[pl.ds(2 * zz, 64, 8), :]
            lower = low_lanes(odd.shape)
            own_ref[2 * p, 64 * zz : 64 * zz + 64] = jnp.where(lower, odd, swap(even))
            own_ref[2 * p + 1, 64 * zz : 64 * zz + 64] = jnp.where(lower, swap(odd), even)
    fine_sends(own_ref, first_ref, second_ref, middle)


def fine_weight_rows(weight_ref, out_ref):
    taps = []
    for at in range(0, 1728, 128):
        part = weight_ref[:, at : min(at + 128, 1728)]
        turned = jnp.concatenate([part, part], axis=0).T
        taps += [turned[r : r + 64] for r in range(0, turned.shape[0], 64)]
    nothing = jnp.zeros((64, 128), F32)
    lower = low_lanes((64, 128))
    for j in range(3):
        for z in range(4):
            across = []
            for i in range(3):
                at = 3 * (3 * i + j) + z
                odd = taps[at - 1] if z >= 1 else nothing
                even = taps[at] if z <= 2 else nothing
                across.append(jnp.where(lower, odd, even))
            for n, part in enumerate(filter_taps(*across)):
                h, l = split(part)
                at = 768 * n + 256 * j + 64 * z
                out_ref[at : at + 64, 0:128] = h
                out_ref[at : at + 64, 128:256] = l


def coarse_weight_rows(weight_ref, out_ref):
    for n in range(9):
        taps = [weight_ref[:, 128 * t : 128 * t + 128].T for t in range(3 * n, 3 * n + 3)]
        for k, part in enumerate(filter_taps(*taps)):
            h, l = split(part)
            at = 1152 * k + 128 * n
            out_ref[at : at + 128, 0:128] = h
            out_ref[at : at + 128, 128:256] = l


def fine_weight_kernel(weight_ref, out_ref):
    fine_weight_rows(weight_ref, out_ref)


def down_weights_kernel(first_ref, down_ref, first_out, down_out):
    coarse_weight_rows(first_ref, first_out)
    nothing = jnp.zeros((64, 128), F32)
    for k, rows in enumerate(([down_ref[...], nothing], [nothing, down_ref[...]])):
        h, l = split(jnp.concatenate(rows, axis=0))
        down_out[:, 128 * k : 128 * k + 128] = h
        down_out[:, 256 + 128 * k : 384 + 128 * k] = l


def up_weights_kernel(second_ref, up_ref, second_out, up_out):
    coarse_weight_rows(second_ref, second_out)
    both = jnp.concatenate([up_ref[...], up_ref[...]], axis=0).T
    lower = low_lanes(both.shape)
    for k in range(2):
        h, l = split(jnp.where(lower if k == 0 else ~lower, both, 0.0))
        up_out[128 * k : 128 * k + 128, 0:128] = h
        up_out[128 * k : 128 * k + 128, 128:256] = l


def fine_in_kernel(
    codes_ref, links_ref, coarse_links_ref, own_ref, first_ref, second_ref, weight_ref, bias_ref,
    hidden_ref, pooled_ref, source, high, low, sums, middle,
):
    source[8] = jnp.zeros((256, 128), F32)
    source[2:6] = own_ref[...]
    fine_halo(first_ref, second_ref, source, middle)
    fine_rim(source, links_ref, high, low)
    bias = jnp.concatenate([bias_ref[...]] * 2, axis=1)
    for half in range(2):
        r = silu(fine_convolved(high, low, half, weight_ref, bias))
        for h in range(2):
            at = 64 * (2 * half + h)
            for b in range(4):
                hidden_ref[b, at : at + 64] = r[h, :, 8 * b : 8 * b + 8].reshape(64, 128)
        r = r.reshape(2, 4, 2, 32, 128)
        r = r[:, :, 0] + r[:, :, 1]
        r = r + swap(r)
        both = jnp.where(low_lanes(r[0].shape), r[1], r[0])
        sums[128 * half : 128 * half + 128, :] = both.reshape(128, 128)
    means = (sums[pl.ds(0, 128, 2), :] + sums[pl.ds(1, 128, 2), :]) * 0.125
    for n in range(8):
        for b in range(4):
            at = (4 * n + b) * 4
            pooled_ref[0, 32 * b + 4 * n : 32 * b + 4 * n + 4, :] = means[at : at + 4]
    lane = lax.broadcasted_iota(jnp.int32, (8, 128), 1)
    named = jnp.zeros((8, 128), F32)
    for b in range(4):
        named = jnp.where(lane == b, codes_ref[b].astype(F32), named)
    pooled_ref[0, 128:136, :] = named
    pooled_ref[0, 129:131, 0:26] = coarse_links_ref[...].astype(F32)
    for k in range(1, 16):
        pooled_ref[k] = pooled_ref[0]


def cube_rows(all_ref, place_ref, code, store):
    for t in range(16):
        a, b, c = t // 4 % 2, t // 2 % 2, t % 2
        i = place_ref[code + t]
        at = jnp.maximum(i, 0)
        v = all_ref[at // 4, pl.ds(pl.multiple_of(at % 4 * 32, 32), 32), :]
        v = jnp.where(i >= 0, v, 0.0)
        for r in range(8):
            store(t // 8, (2 * c + r // 4) * 64 + (4 * a + r % 4) * 8 + 4 * b, v[4 * r : 4 * r + 4])


def edge_kernel(all_ref, cubes_ref, place_ref, codes_ref, held, spelled, cubes, middle, sem):
    held[...] = all_ref[:, 128, :]
    copy = pltpu.make_async_copy(held, spelled, sem)
    copy.start()
    me = lax.axis_index("dev")
    for t in range(256):
        place_ref[t] = -1
    copy.wait()
    for i in range(64):
        code = spelled[i // 4, i % 4].astype(jnp.int32)
        codes_ref[i] = code
        place_ref[code] = i
    cubes_ref[832:840] = all_ref[jnp.where(me < 8, 15, 0), 128:136, :]

    @pl.when((me < 2) | (me > 13))
    def _():
        def store(s, at, v):
            cubes_ref[256 * s + at : 256 * s + at + 4, :] = v

        cube_rows(all_ref, place_ref, jnp.where(me < 2, 15, 0) * 16, store)

        def hold(s, at, v):
            cubes[s, at : at + 4, :] = v

        cube_rows(all_ref, place_ref, jnp.where(me < 2, 14, 1) * 16, hold)
        for s in range(2):
            fine_pack(cubes.at[s], cubes_ref.at[512 + 160 * s : 672 + 160 * s], middle)


def bring_down(cubes, down_ref, source, n):
    h, l = split(cubes)
    based = product(h, l, down_ref[...])
    for z in range(8):
        k = 1 - z % 2
        source[n, 64 * z : 64 * z + 64] = based[64 * (z // 2) : 64 * (z // 2) + 64, 128 * k : 128 * k + 128]


def base_kernel(all_ref, place_ref, down_ref, out_ref, links_ref, cubes):
    me = lax.axis_index("dev")
    links_ref[...] = jnp.zeros((8, 128), F32)
    out_ref[10] = jnp.zeros((512, 128), F32)
    for n in range(5):
        owner = jnp.clip(me + (n - 2), 0, 15)

        def store(s, at, v):
            cubes[s, at : at + 4, :] = v

        cube_rows(all_ref, place_ref, owner * 16, store)
        for s in range(2):
            bring_down(cubes[s], down_ref, out_ref, 2 * n + s)
        if 1 <= n <= 3:
            links_ref[2 * n - 2 : 2 * n] = all_ref[owner, 129:131, :]


def coarse_rim(source, links_ref, row, home, start, none, high, low):
    found = []
    for s in range(2):
        near = neighbours(links_ref, row + s, start, none)
        near[0, 0, 0] = home + s
        found.append(near)
    for dx, at, count, room in CHUNKS:
        window = []
        for z in range(10):
            dz = -1 if z == 0 else 1 if z == 9 else 0
            begin = 64 * {-1: 7, 0: z - 1, 1: 0}[dz] + at
            rows = [
                shifted_rows(
                    lambda dy, near=near: source[near[dx, dy, dz], begin : begin + 8 * count, :].reshape(count, 8, 128)
                )
                for near in found
            ]
            window.append([jnp.concatenate([rows[0][j], rows[1][j]], axis=1) for j in range(3)])
            if z >= 3 and z % 2 == 1:
                for j in range(3):
                    for k, part in enumerate(filter_data(*[w[j] for w in window[z - 3 :]])):
                        h, l = split(part)
                        high[k, j, z // 2 - 1, room : room + count] = h
                        low[k, j, z // 2 - 1, room : room + count] = l


def coarse_convolved(high, low, half, weight_ref, bias):
    def columns(padded, k):
        return jnp.concatenate(
            [
                padded[k, j, 2 * half : 2 * half + 2, i : i + 8].reshape(256, 128)
                for i in range(3)
                for j in range(3)
            ],
            axis=1,
        )

    return [silu(y + bias) for y in filtered(high, low, columns, weight_ref)]


def coarse_first_pair(source, links_ref, pair, weight_ref, bias_ref, out_ref, n, high, low):
    coarse_rim(source, links_ref, 2 * pair, 2 * pair + 2, device_number() * 2 - 4, 10, high, low)
    for half in range(2):
        for odd, r in enumerate(coarse_convolved(high, low, half, weight_ref, bias_ref[...])):
            r = r.reshape(2, 8, 16, 128)
            for s in range(2):
                for h in range(2):
                    at = 64 * (4 * half + 2 * h + odd)
                    out_ref[n + s, at : at + 64] = r[h, :, 8 * s : 8 * s + 8].reshape(64, 128)


def inner_pair():
    return jnp.where(lax.axis_index("dev") < 8, 2, 0)


def inner_kernel(links_ref, based_ref, weight_ref, bias_ref, out_ref, high, low):
    coarse_first_pair(based_ref, links_ref, inner_pair(), weight_ref, bias_ref, out_ref, 0, high, low)


def coarse_kernel(
    links_ref, near_links_ref, codes_ref, based_ref, edge_ref, inner_ref, down_ref, first_weight_ref, first_bias_ref,
    weight_ref, bias_ref, up_ref, out_ref, source, high, low, seconds, high2, low2, octants, held, spelled,
    cubes, middle, sem,
):
    me = lax.axis_index("dev")
    held[...] = near_links_ref[...]

    @pl.when(me == 0)
    def _():
        held[0:2] = edge_ref[833:835]

    @pl.when(me == 15)
    def _():
        held[4:6] = edge_ref[833:835]

    copy = pltpu.make_async_copy(held, spelled, sem)
    copy.start()
    source[...] = based_ref[...]

    @pl.when((me < 2) | (me > 13))
    def _():
        at = jnp.where(me < 2, jnp.where(me == 0, 2, 0), jnp.where(me == 15, 6, 8))
        for s in range(2):
            bring_down(edge_ref[256 * s : 256 * s + 256], down_ref, source, at + s)

    @pl.when((me == 0) | (me == 15))
    def _():
        at = jnp.where(me == 0, 0, 8)
        for s in range(2):
            fine_unpack(edge_ref.at[512 + 160 * s : 672 + 160 * s], cubes, middle)
            bring_down(cubes[...], down_ref, source, at + s)

    seconds[6] = jnp.zeros((512, 128), F32)
    inner = inner_pair()
    for s in range(2):
        seconds[2 * inner + s] = inner_ref[s]
    copy.wait()
    outer = 2 - inner
    coarse_first_pair(source, spelled, outer, first_weight_ref, first_bias_ref, seconds, 2 * outer, high, low)
    coarse_first_pair(source, spelled, 1, first_weight_ref, first_bias_ref, seconds, 2, high2, low2)
    coarse_rim(seconds, links_ref, 0, 2, device_number() * 2 - 2, 6, high, low)
    for c in range(2):
        h, l = split(jnp.concatenate(coarse_convolved(high, low, c, weight_ref, bias_ref[...]), axis=1))
        lifted = product(h, l, up_ref[...])
        for t in range(c, 16, 2):
            s, a, b = t // 8, t // 4 % 2, t // 2 % 2
            for q in range(2):
                for x in range(4):
                    at = 128 * q + (4 * a + x) * 16 + 8 * s + 4 * b
                    octants[t, 16 * q + 4 * x : 16 * q + 4 * x + 4, :] = lifted[at : at + 4]
    base = lax.axis_index("dev") * 16

    def place(i, carry):
        local = codes_ref[i] - base
        known = (local >= 0) & (local < 16)
        v = octants[jnp.clip(local, 0, 15)]
        out_ref[i] = jnp.where(known, v, 0.0)
        return carry

    lax.fori_loop(0, 64, place, 0)


def blend_kernel(hidden_ref, risen_ref, out_ref, first_ref, second_ref, grown, middle):
    risen = risen_ref[0]
    for k in range(1, 16):
        risen = risen + risen_ref[k]
    for b in range(4):
        v = risen[32 * b : 32 * b + 32]
        grown[pl.ds(0, 32, 2), :] = v
        grown[pl.ds(1, 32, 2), :] = v
        full = grown[...].reshape(2, 4, 1, 8, 128)
        turned = swap(full)
        lower = low_lanes(full.shape)
        for h in range(2):
            w = jnp.where(lower, full, turned) if h == 0 else jnp.where(lower, turned, full)
            for q in range(2):
                at = 64 * (2 * q + h)
                v = silu(hidden_ref[b, at : at + 64].reshape(4, 2, 8, 128) + w[q])
                out_ref[b, at : at + 64] = v.reshape(64, 128)
    fine_sends(out_ref, first_ref, second_ref, middle)


def fine_out_kernel(
    links_ref, own_ref, second_ref, first_ref, features_ref, weight_ref, bias_ref,
    out_ref, source, flat, high, low, middle,
):
    source[8] = jnp.zeros((256, 128), F32)
    source[2:6] = own_ref[...]
    fine_halo(first_ref, second_ref, source, middle)
    fine_rim(source, links_ref, high, low)
    bias = jnp.concatenate([bias_ref[...]] * 2, axis=1)
    for zz in range(4):
        if zz % 2 == 0:
            both = fine_convolved(high, low, zz // 2, weight_ref, bias)
        r = both[zz % 2]
        for p in range(2):
            v0 = r[:, 16 * p : 16 * p + 8].reshape(64, 128)
            v1 = r[:, 16 * p + 8 : 16 * p + 16].reshape(64, 128)
            lower = low_lanes(v0.shape)
            flat[p, pl.ds(2 * zz + 1, 64, 8), :] = jnp.where(lower, v0, swap(v1))
            flat[p, pl.ds(2 * zz, 64, 8), :] = jnp.where(lower, swap(v0), v1)
    for p in range(2):
        out_ref[2 * p : 2 * p + 2] = features_ref[2 * p : 2 * p + 2] + flat[p].T.reshape(2, 64, 512)


def exchanged(first, second):
    count = lax.axis_size(BOTH)
    inner = [(i, i ^ 1) for i in range(count)]
    outer = [(i, i + 1) for i in range(1, count - 1, 2)]
    outer += [(b, a) for a, b in outer]
    second = lax.ppermute(second, BOTH, outer)
    return lax.ppermute(first, BOTH, inner), second


def struct(*shape, dtype=F32):
    return jax.ShapeDtypeStruct(shape, dtype)


def call(kernel, out, scratch, specs, args, flops):
    return pl.pallas_call(
        kernel,
        out_shape=out,
        in_specs=specs,
        out_specs=jax.tree.map(lambda o: SMEM if o.dtype == jnp.int32 else VMEM, out),
        scratch_shapes=scratch,
        cost_estimate=pl.CostEstimate(flops=flops, bytes_accessed=1 << 21, transcendentals=0),
        compiler_params=pltpu.CompilerParams(vmem_limit_bytes=40 << 20),
    )(*args)


def per_device(
    features, fine_links, codes, coarse_links, fine_in_weight, fine_in_bias, down_weight,
    coarse_first_weight, coarse_first_bias, coarse_second_weight, coarse_second_bias,
    up_weight, fine_out_weight, fine_out_bias,
):
    fine_padded = [pltpu.VMEM((4, 3, 5, 4, 32, 128), BF16)] * 2
    fine_source = pltpu.VMEM((9, 256, 128), F32)
    middle = pltpu.VMEM((192, 128), F32)
    brick, shell = struct(4, 256, 128), struct(2, 160, 128)

    own, first, second = call(
        turn_kernel,
        (brick, shell, shell),
        [pltpu.VMEM((512, 128), F32), middle],
        [VMEM],
        (features,),
        1 << 20,
    )
    first, second = exchanged(first, second)
    fine_rows, coarse_rows = struct(3072, 256, dtype=BF16), struct(4608, 256, dtype=BF16)
    weight_in = call(fine_weight_kernel, fine_rows, [], [VMEM], (fine_in_weight,), 1 << 20)
    weight_first, down = call(
        down_weights_kernel,
        (coarse_rows, struct(128, 512, dtype=BF16)),
        [],
        [VMEM] * 2,
        (coarse_first_weight, down_weight.T),
        1 << 20,
    )
    weight_second, up = call(
        up_weights_kernel,
        (coarse_rows, struct(256, 256, dtype=BF16)),
        [],
        [VMEM] * 2,
        (coarse_second_weight, up_weight),
        1 << 20,
    )
    weight_in, weight_first, down, weight_second, up = lax.optimization_barrier(
        (weight_in, weight_first, down, weight_second, up)
    )
    hidden, pooled = call(
        fine_in_kernel,
        (brick, struct(16, 136, 128)),
        [fine_source, *fine_padded, pltpu.VMEM((256, 128), F32), middle],
        [SMEM, SMEM] + [VMEM] * 6,
        (codes, fine_links, coarse_links, own, first, second, weight_in, fine_in_bias[None]),
        2 * 1024 * 2304 * 384,
    )
    spread = lax.all_to_all(pooled, "dev", 0, 0, tiled=True)
    cubes, place, group_codes = call(
        edge_kernel,
        (struct(840, 128), struct(256, dtype=jnp.int32), struct(64, dtype=jnp.int32)),
        [
            pltpu.VMEM((16, 128), F32), pltpu.SMEM((16, 128), F32), pltpu.VMEM((2, 256, 128), F32),
            middle, pltpu.SemaphoreType.DMA,
        ],
        [VMEM],
        (spread,),
        1 << 20,
    )
    groups, devices = lax.axis_size("grp"), lax.axis_size("dev")
    edges = [(g * devices + k, (g + 1) * devices + k) for g in range(groups - 1) for k in (0, 1)]
    edges += [((g + 1) * devices + k, g * devices + k) for g in range(groups - 1) for k in (14, 15)]
    edge = lax.ppermute(cubes, BOTH, edges)
    based, near_links = call(
        base_kernel,
        (struct(11, 512, 128), struct(8, 128)),
        [pltpu.VMEM((2, 256, 128), F32)],
        [VMEM, SMEM, VMEM],
        (spread, place, down),
        1 << 28,
    )
    coarse_padded = [pltpu.VMEM((4, 3, 4, 10, 16, 128), BF16)] * 2
    inner = call(
        inner_kernel,
        struct(2, 512, 128),
        coarse_padded,
        [SMEM] + [VMEM] * 3,
        (near_links, based, weight_first, coarse_first_bias[None]),
        2 * 1024 * 3456 * 384,
    )
    lifted = call(
        coarse_kernel,
        struct(64, 32, 128),
        [
            pltpu.VMEM((11, 512, 128), F32), *coarse_padded, pltpu.VMEM((7, 512, 128), F32), *coarse_padded,
            pltpu.VMEM((16, 32, 128), F32), pltpu.VMEM((8, 128), F32), pltpu.SMEM((8, 128), F32),
            pltpu.VMEM((256, 128), F32), middle, pltpu.SemaphoreType.DMA,
        ],
        [SMEM, VMEM, SMEM] + [VMEM] * 9,
        (
            coarse_links, near_links, group_codes, based, edge, inner, down, weight_first,
            coarse_first_bias[None], weight_second, coarse_second_bias[None], up,
        ),
        6 * 1024 * 3456 * 384,
    )
    risen = lax.all_to_all(lifted.reshape(16, 128, 128), "dev", 0, 0, tiled=True)
    blended, first, second = call(
        blend_kernel,
        (brick, shell, shell),
        [pltpu.VMEM((64, 128), F32), middle],
        [VMEM, VMEM],
        (hidden, risen),
        1 << 20,
    )
    first, second, out_raw = lax.optimization_barrier((first, second, fine_out_weight))
    weight_out = call(fine_weight_kernel, fine_rows, [], [VMEM], (out_raw,), 1 << 20)
    first, second = exchanged(first, second)
    return call(
        fine_out_kernel,
        struct(4, 64, 512),
        [fine_source, pltpu.VMEM((2, 512, 128), F32), *fine_padded, middle],
        [SMEM] + [VMEM] * 6,
        (fine_links, blended, second, first, features, weight_out, fine_out_bias[None]),
        2 * 1024 * 2304 * 384,
    )


def solution(mesh):
    split_first = P(BOTH)
    placed = (split_first,) * 4 + (P(),) * 10
    return jax.shard_map(
        per_device,
        mesh=mesh,
        in_specs=placed,
        out_specs=split_first,
        check_vma=False,
    )
```
